128 devices in a mesh: lat: 16 (over z_lo, y, core), lon: 8 (over z_hi, x).
Axes of the slice: x: 4, y: 4, z: 4 (z_hi: 2, z_lo: 2; z = z_hi * 2 + z_lo), core: 2. Of those that a mesh axis runs over, the one named last changes fastest.
Arguments:
- tokens: bfloat16 [192, 192, 2, 512], P('lat', 'lon'), may hold values from -6 to 6
- fine_qkv: bfloat16 [512, 1536], replicated
- fine_proj: bfloat16 [512, 512], replicated, may hold values from -0.25 to 0.25
- fine_up: bfloat16 [512, 2048], replicated, may hold values from -0.25 to 0.25
- fine_down: bfloat16 [2048, 512], replicated, may hold values from -0.125 to 0.125
- merge_weight: bfloat16 [2048, 1024], replicated, may hold values from -0.125 to 0.125
- coarse_qkv: bfloat16 [1024, 3072], replicated
- coarse_proj: bfloat16 [1024, 1024], replicated, may hold values from -0.1875 to 0.1875
- cotangent: float32 [96, 96, 2, 1024], P('lat', 'lon'), may hold values from -6 to 6
Outputs:
- coarse_out: bfloat16 [96, 96, 2, 1024], P('lat', 'lon')
- input_grad: float32 [192, 192, 2, 512], P('lat', 'lon')
- proj_grad: float32 [1024, 1024], replicated
The draws below stay inside these ranges and needn't reach their ends.
All inputs are finite; a program needn't handle non-finite values.
Results may differ from the reference program's by a relative error of at most 0.0365.
Values may be sent and summed in bfloat16 or wider, within the bound.
No kernel may reach another device: no remote copies, remote signals or barrier semaphores. Data moves between devices by JAX's collectives and lax.ppermute only.
A program may use at most 192 MiB of HBM per device.

```python
import jax
import jax.numpy as jnp
from jax import lax

FINE_WIDTH = 512
COARSE_WIDTH = 1024
FINE_HEADS = 8
COARSE_HEADS = 16
FINE_HIDDEN = 2048
WIN_LAT = 6
WIN_LON = 12
LEVELS = 2
LAT_CELLS = 192
LON_CELLS = 192


def draw_fine_qkv(key, part):
    key = jax.random.fold_in(key, 11)
    normal_part = jax.random.normal(key, (FINE_WIDTH, 3 * FINE_WIDTH), jnp.float32) * FINE_WIDTH ** (-0.5)
    return normal_part.astype(jnp.bfloat16)


def draw_coarse_qkv(key, part):
    key = jax.random.fold_in(key, 23)
    normal_part = jax.random.normal(key, (COARSE_WIDTH, 3 * COARSE_WIDTH), jnp.float32) * COARSE_WIDTH ** (-0.5)
    return normal_part.astype(jnp.bfloat16)


def shard_levels(stream_key, extent, shards, low, largest):
    gain, own = 1.0, jax.random.fold_in(stream_key, 6)
    for dim, parts in shards:
        heights = jnp.exp(jax.random.uniform(jax.random.fold_in(own, dim), (parts,), jnp.float32, low / len(shards), largest / len(shards)))
        gain = gain * jnp.repeat(heights, extent[dim] // parts).reshape([-1 if axis == dim else 1 for axis in range(len(extent))])
    return gain


def gaussian(stream_key, shape, deviation, bound, pieces=(), held_as=jnp.bfloat16):
    array = jax.random.normal(stream_key, shape, jnp.float32) * deviation
    if len(pieces) > 0:
        array = shard_levels(stream_key, shape, pieces, -0.22, 0.18) * array
    return jnp.clip(array, min=-bound, max=bound).astype(held_as)


def setup_inputs(seed: int = 0) -> dict:
    keys = jax.random.split(jax.random.key(seed), 10)
    tokens = gaussian(keys[0], (LAT_CELLS, LON_CELLS, LEVELS, FINE_WIDTH), 1.0, 6.0, ((0, 16), (1, 8)))
    fine_qkv = draw_fine_qkv(jax.random.fold_in(keys[9], 71), 0)
    fine_proj = gaussian(keys[2], (FINE_WIDTH, FINE_WIDTH), FINE_WIDTH ** -0.5, 0.25)
    fine_up = gaussian(keys[3], (FINE_WIDTH, FINE_HIDDEN), FINE_WIDTH ** -0.5, 0.25)
    fine_down = gaussian(keys[4], (FINE_HIDDEN, FINE_WIDTH), FINE_HIDDEN ** -0.5, 0.125)
    merge_weight = gaussian(keys[5], (4 * FINE_WIDTH, COARSE_WIDTH), (4 * FINE_WIDTH) ** -0.5, 0.125)
    coarse_qkv = draw_coarse_qkv(jax.random.fold_in(keys[9], 71), 0)
    coarse_proj = gaussian(keys[7], (COARSE_WIDTH, COARSE_WIDTH), COARSE_WIDTH ** -0.5, 0.1875)
    cotangent = gaussian(keys[8], (LAT_CELLS // 2, LON_CELLS // 2, LEVELS, COARSE_WIDTH), 1.0, 6.0, ((0, 16), (1, 8)), jnp.float32)
    return {"tokens": tokens, "fine_qkv": fine_qkv, "fine_proj": fine_proj, "fine_up": fine_up, "fine_down": fine_down, "merge_weight": merge_weight, "coarse_qkv": coarse_qkv, "coarse_proj": coarse_proj, "cotangent": cotangent}


eps_norm = 1e-05

def layer_norm(values):
    average = lax.optimization_barrier(jnp.mean(values, axis=-1, keepdims=True))
    centered = values - average
    spread = lax.optimization_barrier(jnp.mean(centered * centered, axis=-1, keepdims=True))
    return centered * lax.rsqrt(spread + eps_norm)

def window_block(padded, qkv_weight, proj_weight, head_count, lat_start, lat_total, win_lat, win_lon):
    lat_rows, lon_cols, levels, channels = padded.shape
    head_dim = channels // head_count
    blocks_lat = lat_rows // win_lat
    blocks_lon = lon_cols // win_lon
    normed = layer_norm(padded).astype(jnp.bfloat16)
    packed = jnp.dot(normed.reshape(-1, channels), qkv_weight, preferred_element_type=jnp.float32).astype(jnp.bfloat16)
    packed = packed.reshape(blocks_lat, win_lat, blocks_lon, win_lon, levels, 3, head_count, head_dim)
    packed = packed.transpose(5, 0, 2, 6, 1, 3, 4, 7).reshape(3, blocks_lat * blocks_lon, head_count, win_lat * win_lon * levels, head_dim)
    queries, key_part, value_part = (packed[0], packed[1], packed[2])
    scores = jnp.einsum('nhsd,nhtd->nhst', queries, key_part, preferred_element_type=jnp.float32) * head_dim ** (-0.5)
    row_ids = lat_start + jnp.arange(lat_rows, dtype=jnp.int32)
    inside = (row_ids >= 0) & (row_ids < lat_total)
    inside = jnp.broadcast_to(inside.reshape(blocks_lat, 1, win_lat, 1, 1), (blocks_lat, blocks_lon, win_lat, win_lon, levels))
    inside = inside.reshape(blocks_lat * blocks_lon, 1, 1, win_lat * win_lon * levels)
    scores = jnp.where(inside, scores, -1e+30)
    highest = lax.optimization_barrier(jnp.max(scores, axis=-1, keepdims=True))
    weights = jnp.exp(scores - highest)
    attention = (weights / lax.optimization_barrier(jnp.sum(weights, axis=-1, keepdims=True))).astype(jnp.bfloat16)
    combined = jnp.einsum('nhst,nhtd->nhsd', attention, value_part, preferred_element_type=jnp.float32).astype(jnp.bfloat16)
    combined = combined.reshape(blocks_lat, blocks_lon, head_count, win_lat, win_lon, levels, head_dim)
    combined = combined.transpose(0, 3, 1, 4, 5, 2, 6).reshape(-1, channels)
    projected = jnp.dot(combined.astype(proj_weight.dtype), proj_weight, preferred_element_type=jnp.float32)
    return padded + projected.reshape(lat_rows, lon_cols, levels, channels)

def feed_forward(field, up_weight, down_weight):
    lat_rows, lon_cols, levels, channels = field.shape
    normed = layer_norm(field).astype(jnp.bfloat16).reshape(-1, channels)
    hidden = jnp.dot(normed, up_weight, preferred_element_type=jnp.float32)
    hidden = jax.nn.gelu(hidden, approximate=False).astype(jnp.bfloat16)
    lowered = jnp.dot(hidden, down_weight, preferred_element_type=jnp.float32)
    return field + lowered.reshape(lat_rows, lon_cols, levels, channels)

def merge_block(field, merge_weight):
    lat_rows, lon_cols, levels, channels = field.shape
    grouped = field.reshape(lat_rows // 2, 2, lon_cols // 2, 2, levels, channels)
    grouped = grouped.transpose(0, 2, 4, 1, 3, 5).reshape(-1, 4 * channels)
    normed = layer_norm(grouped).astype(jnp.bfloat16)
    merged = jnp.dot(normed, merge_weight, preferred_element_type=jnp.float32)
    return merged.reshape(lat_rows // 2, lon_cols // 2, levels, merge_weight.shape[1])

def centre(field, half_lat, half_lon):
    return field[half_lat:field.shape[0] - half_lat, half_lon:field.shape[1] - half_lon]

def fine_attention(field, qkv_weight, proj_weight):
    half_lat = WIN_LAT // 2
    half_lon = WIN_LON // 2
    widened = jnp.concatenate([field[:, -half_lon:], field, field[:, :half_lon]], axis=1)
    padded = jnp.pad(widened, ((half_lat, half_lat), (0, 0), (0, 0), (0, 0)))
    whole_out = window_block(padded, qkv_weight, proj_weight, FINE_HEADS, -half_lat, field.shape[0], WIN_LAT, WIN_LON)
    return centre(whole_out, half_lat, half_lon)

def reference(tokens, fine_qkv, fine_proj, fine_up, fine_down, merge_weight, coarse_qkv, coarse_proj, cotangent):
    tokens_f = tokens.astype(jnp.float32)
    attended, pull_attend = jax.vjp(lambda field: fine_attention(field, fine_qkv, fine_proj), tokens_f)
    fine_full, pull_forward = jax.vjp(lambda field: feed_forward(field, fine_up, fine_down), attended)
    fine_out = lax.optimization_barrier(fine_full.astype(jnp.bfloat16)).astype(jnp.float32)
    merged_full, pull_merge = jax.vjp(lambda field: merge_block(field, merge_weight), fine_out)
    merged = lax.optimization_barrier(merged_full.astype(jnp.bfloat16)).astype(jnp.float32)
    coarse_rows = merged.shape[0]

    def coarse_attention(field, proj_float):
        return window_block(field, coarse_qkv, proj_float, COARSE_HEADS, 0, coarse_rows, WIN_LAT, WIN_LON)
    coarse_full, pull_coarse = jax.vjp(coarse_attention, merged, coarse_proj.astype(jnp.float32))
    merged_grad, proj_total = pull_coarse(cotangent)
    cell_count = merged.shape[0] * merged.shape[1] * merged.shape[2]
    proj_grad = proj_total * float(cell_count) ** (-0.5)
    fine_grad = pull_merge(merged_grad)[0]
    attended_grad = pull_forward(fine_grad)[0]
    input_grad = pull_attend(attended_grad)[0]
    return (coarse_full.astype(jnp.bfloat16), input_grad, proj_grad)
```

```python
import jax
import jax.numpy as jnp
import numpy as np
from jax import lax
from jax.experimental import pallas as pl
from jax.experimental.pallas import tpu as pltpu
from jax.sharding import PartitionSpec as P

BF = jnp.bfloat16
F32 = jnp.float32
ROWS = 12
COLS = 24
CELLS = ROWS * COLS * 2
WIN = 144
HALF_LAT = 3
HALF_LON = 6
FINE = 512
COARSE = 1024
HIDDEN = 2048
QUAD = 256
CHUNK = 512
PIECES = (336, 112, 112, 48)
PACKED = sum(PIECES)
EPS = 1e-05
BOTH = ("lat", "lon")


def cell_orders():
    number = np.arange(CELLS).reshape(ROWS, COLS, 2)
    r, c = ROWS - HALF_LAT, COLS - HALF_LON
    parts = (number[:r, :c], number[:r, c:], number[r:, :c], number[r:, c:])
    pieces = np.full(PACKED, -1)
    start = 0
    for part, room in zip(parts, PIECES):
        pieces[start : start + part.size] = part.reshape(-1)
        start += room
    parity = number.reshape(6, 2, 12, 2, 2).transpose(1, 3, 0, 2, 4).reshape(-1)
    place = np.zeros(CELLS, int)
    place[pieces[pieces >= 0]] = np.nonzero(pieces >= 0)[0]
    place = place.reshape(ROWS, COLS, 2)
    rolled = np.roll(place, (HALF_LAT, HALF_LON), (0, 1))
    window = rolled.reshape(2, 6, 2, 12, 2).transpose(0, 2, 1, 3, 4).reshape(-1)
    return pieces, parity, window


def selector(sources, width):
    matrix = np.zeros((len(sources), width), np.float32)
    for row, source in enumerate(sources):
        if source >= 0:
            matrix[row, source] = 1.0
    return matrix.astype(jnp.bfloat16)


PIECE_CELLS, PARITY_CELLS, WINDOW_PLACES = cell_orders()
PLACE_OF = np.zeros(CELLS, int)
PLACE_OF[PIECE_CELLS[PIECE_CELLS >= 0]] = np.nonzero(PIECE_CELLS >= 0)[0]
GATHER_PIECES = selector(PIECE_CELLS, CELLS)
WINDOW_FROM_PIECES = selector(WINDOW_PLACES, PACKED)
PIECES_FROM_WINDOW = np.ascontiguousarray(WINDOW_FROM_PIECES.T)
PARITY_FROM_PIECES = selector(PLACE_OF[PARITY_CELLS], PACKED)
PIECES_FROM_PARITY = np.ascontiguousarray(PARITY_FROM_PIECES.T)
CELLS_FROM_PIECES = selector(PLACE_OF, PACKED)


def mm(a, b):
    return jnp.dot(a, b, preferred_element_type=F32)


def mm_nt(a, b):
    return lax.dot_general(a, b, (((1,), (1,)), ((), ())), preferred_element_type=F32)


def mm_tn(a, b):
    return lax.dot_general(a, b, (((0,), (0,)), ((), ())), preferred_element_type=F32)


def normed(values):
    centered = values - jnp.mean(values, axis=-1, keepdims=True)
    scale = lax.rsqrt(jnp.mean(centered * centered, axis=-1, keepdims=True) + EPS)
    return centered * scale, scale


def normed_pull(unit, scale, grad):
    low = jnp.mean(grad, axis=-1, keepdims=True)
    along = jnp.mean(grad * unit, axis=-1, keepdims=True)
    return scale * (grad - low - unit * along)


def heads_apart(values):
    head = lax.broadcasted_iota(jnp.int32, values.shape, 1) // 64
    zero = jnp.zeros_like(values)
    return jnp.concatenate([jnp.where(head == h, values, zero) for h in range(4)], axis=0)


def heads_joined(stacked):
    rows = stacked.shape[0] // 4
    head = lax.broadcasted_iota(jnp.int32, (rows, QUAD), 1) // 64
    out = stacked[:rows]
    for h in range(1, 4):
        out = jnp.where(head == h, stacked[h * rows : (h + 1) * rows], out)
    return out


def attend(q, k, v, bias):
    apart = heads_apart(q * 0.125)
    scores = mm_nt(apart, k)
    if bias is not None:
        scores = scores + bias
    weights = jnp.exp(scores - jnp.max(scores, axis=-1, keepdims=True))
    a = (weights * (1.0 / jnp.sum(weights, axis=-1, keepdims=True))).astype(BF)
    return a, heads_joined(mm(a, v)).astype(BF)


def attend_pull(q, k, v, a, grad):
    apart = heads_apart(grad)
    af = a.astype(F32)
    weighted = mm_nt(apart, v) * af
    ds = (weighted - af * jnp.sum(weighted, axis=-1, keepdims=True)).astype(BF)
    dq = heads_joined(mm(ds, k)) * 0.125
    dk = mm_tn(ds, heads_apart(q * 0.125))
    dv = mm_tn(a, apart)
    return dq.astype(BF), dk.astype(BF), dv.astype(BF)


def gelu_pair(h):
    cdf = 0.5 * (1.0 + lax.erf(h * 0.7071067811865476))
    return h * cdf, cdf + h * (0.3989422804014327 * jnp.exp(-0.5 * h * h))


def split_pieces(packed, refs):
    start = 0
    for ref, room in zip(refs, PIECES):
        ref[...] = packed[start : start + room].astype(ref.dtype)
        start += room


def joined_pieces(refs):
    return jnp.concatenate([ref[...] for ref in refs], axis=0)


def fine_forward(
    edge, keep, beside, above, corner, order, back, qkv_w, proj_w, up_w, down_w,
    out0, out1, out2, out3, x_out, qkv_out, a_out, att_out, slope_out, mixed
):
    x = mm(order[...], joined_pieces((keep, beside, above, corner)))
    x_out[...] = x.astype(BF)
    unit, _ = normed(x)
    qkv_out[...] = mm(unit.astype(BF), qkv_w[...]).astype(BF)
    half_q = (lax.broadcasted_iota(jnp.int32, (4 * WIN, WIN), 0) % WIN) >= WIN // 2
    half_k = lax.broadcasted_iota(jnp.int32, (4 * WIN, WIN), 1) >= WIN // 2
    bias = jnp.where(half_q != half_k, edge[0], 0.0)
    for w in range(4):
        for g in range(2):
            rows, cols = slice(w * WIN, (w + 1) * WIN), g * QUAD
            a, o = attend(
                qkv_out[rows, cols : cols + QUAD],
                qkv_out[rows, FINE + cols : FINE + cols + QUAD],
                qkv_out[rows, 2 * FINE + cols : 2 * FINE + cols + QUAD],
                bias if w < 2 else None,
            )
            a_out[2 * w + g] = a
            mixed[rows, cols : cols + QUAD] = o
    attended = x + mm(mixed[...], proj_w[...])
    att_out[...] = attended
    unit, _ = normed(attended)
    unit = unit.astype(BF)
    total = attended
    for c in range(0, HIDDEN, CHUNK):
        value, slope = gelu_pair(mm(unit, up_w[:, c : c + CHUNK]))
        slope_out[:, c : c + CHUNK] = slope.astype(BF)
        total = total + mm(value.astype(BF), down_w[c : c + CHUNK])
    split_pieces(mm(back[...], total.astype(BF)), (out0, out1, out2, out3))


def coarse_forward(
    core, keep, beside, above, corner, order, merge_w, qkv_w, proj_w,
    out, fine_out, merged_out, qkv_out, a_out, own_half, sent_half, mixed
):
    fine = mm(order[...], joined_pieces((keep, beside, above, corner)))
    fine_out[...] = fine.astype(BF)
    parts = [fine[p * WIN : (p + 1) * WIN] for p in range(4)]
    mean = sum(jnp.sum(part, axis=-1, keepdims=True) for part in parts) / (4 * FINE)
    parts = [part - mean for part in parts]
    spread = sum(jnp.sum(part * part, axis=-1, keepdims=True) for part in parts) / (4 * FINE)
    scale = lax.rsqrt(spread + EPS)
    merged = jnp.zeros((WIN, COARSE), F32)
    for p in range(4):
        merged = merged + mm((parts[p] * scale).astype(BF), merge_w[p * FINE : (p + 1) * FINE])
    merged = merged.astype(BF)
    merged_out[...] = merged
    merged = merged.astype(F32)
    unit, _ = normed(merged)
    qkv_out[...] = mm(unit.astype(BF), qkv_w[...]).astype(BF)
    for g in range(4):
        cols = g * QUAD
        a, o = attend(
            qkv_out[:, cols : cols + QUAD],
            qkv_out[:, COARSE + cols : COARSE + cols + QUAD],
            qkv_out[:, 2 * COARSE + cols : 2 * COARSE + cols + QUAD],
            None,
        )
        a_out[g] = a
        mixed[:, cols : cols + QUAD] = o
    low, high = mixed[:, : COARSE // 2], mixed[:, COARSE // 2 :]
    first = core[0] == 0
    own_half[...] = jnp.where(first, low, high)
    sent_half[...] = jnp.where(first, high, low)
    out[...] = (merged + mm(mixed[...], proj_w[...])).astype(BF)


def proj_partial(own, other, cot_own, cot_other, out):
    total = mm_tn(own[...], cot_own[...]) + mm_tn(other[...], cot_other[...])
    out[...] = (total * 18432.0 ** (-0.5)).astype(BF)


def coarse_backward(
    cot, fine, merged, qkv, a, order, merge_w, qkv_w, proj_w,
    out0, out1, out2, out3, dqkv
):
    grad = mm_nt(cot[...].astype(BF), proj_w[...]).astype(BF)
    for g in range(4):
        cols = g * QUAD
        pulled = attend_pull(
            qkv[:, cols : cols + QUAD],
            qkv[:, COARSE + cols : COARSE + cols + QUAD],
            qkv[:, 2 * COARSE + cols : 2 * COARSE + cols + QUAD],
            a[g],
            grad[:, cols : cols + QUAD],
        )
        for i in range(3):
            dqkv[:, i * COARSE + cols : i * COARSE + cols + QUAD] = pulled[i]
    dn = mm_nt(dqkv[...], qkv_w[...]).astype(BF).astype(F32)
    unit, scale = normed(merged[...].astype(F32))
    merged_grad = (cot[...] + normed_pull(unit, scale, dn)).astype(BF)
    parts = [fine[p * WIN : (p + 1) * WIN].astype(F32) for p in range(4)]
    mean = sum(jnp.sum(part, axis=-1, keepdims=True) for part in parts) / (4 * FINE)
    parts = [part - mean for part in parts]
    spread = sum(jnp.sum(part * part, axis=-1, keepdims=True) for part in parts) / (4 * FINE)
    scale = lax.rsqrt(spread + EPS)
    units = [part * scale for part in parts]
    grads = [
        mm_nt(merged_grad, merge_w[p * FINE : (p + 1) * FINE]).astype(BF).astype(F32)
        for p in range(4)
    ]
    low = sum(jnp.sum(g, axis=-1, keepdims=True) for g in grads) / (4 * FINE)
    along = sum(jnp.sum(g * u, axis=-1, keepdims=True) for g, u in zip(grads, units)) / (4 * FINE)
    fine_grad = jnp.concatenate(
        [(scale * (g - low - u * along)).astype(BF) for g, u in zip(grads, units)], axis=0
    )
    split_pieces(mm(order[...], fine_grad), (out0, out1, out2, out3))


def fine_backward(
    keep, beside, above, corner, order, back, x, qkv, a, att, slope, qkv_w, proj_w, up_w, down_w,
    out0, out1, out2, out3, dqkv
):
    incoming = mm(order[...], joined_pieces((keep, beside, above, corner)))
    rounded = incoming.astype(BF)
    dn = jnp.zeros((CELLS, FINE), F32)
    for c in range(0, HIDDEN, CHUNK):
        dh = mm_nt(rounded, down_w[c : c + CHUNK]) * slope[:, c : c + CHUNK].astype(F32)
        dn = dn + mm_nt(dh.astype(BF), up_w[:, c : c + CHUNK])
    unit, scale = normed(att[...])
    att_grad = incoming + normed_pull(unit, scale, dn)
    grad = mm_nt(att_grad.astype(BF), proj_w[...]).astype(BF)
    for w in range(4):
        for g in range(2):
            rows, cols = slice(w * WIN, (w + 1) * WIN), g * QUAD
            pulled = attend_pull(
                qkv[rows, cols : cols + QUAD],
                qkv[rows, FINE + cols : FINE + cols + QUAD],
                qkv[rows, 2 * FINE + cols : 2 * FINE + cols + QUAD],
                a[2 * w + g],
                grad[rows, cols : cols + QUAD],
            )
            for i in range(3):
                dqkv[rows, i * FINE + cols : i * FINE + cols + QUAD] = pulled[i]
    dn = mm_nt(dqkv[...], qkv_w[...])
    unit, scale = normed(x[...].astype(F32))
    total = att_grad + normed_pull(unit, scale, dn)
    split_pieces(mm(back[...], total.astype(BF)), (out0, out1, out2, out3))


def unpack(keep, beside, above, corner, order, out):
    out[...] = mm(order[...], joined_pieces((keep, beside, above, corner)))


def pack(cells, order, out0, out1, out2, out3):
    split_pieces(mm(order[...], cells[...]), (out0, out1, out2, out3))


def call(body, name, operands, outs, scratch=(), flops=0, scalars=0):
    vmem = pl.BlockSpec(memory_space=pltpu.VMEM)
    smem = pl.BlockSpec(memory_space=pltpu.SMEM)
    moved = sum(int(np.prod(o.shape)) * o.dtype.itemsize for o in jax.tree.leaves((operands, outs)))
    return pl.pallas_call(
        body,
        name=name,
        out_shape=outs,
        in_specs=[smem] * scalars + [vmem] * (len(operands) - scalars),
        out_specs=jax.tree.map(lambda _: vmem, outs),
        scratch_shapes=list(scratch),
        compiler_params=pltpu.CompilerParams(vmem_limit_bytes=60 * 2**20),
        cost_estimate=pl.CostEstimate(flops=flops, bytes_accessed=moved, transcendentals=0),
    )(*operands)


def piece_shapes():
    return [jax.ShapeDtypeStruct((room, FINE), BF) for room in PIECES]


def shifted(pieces, sign):
    lat_count, lon_count = lax.axis_size("lat"), lax.axis_size("lon")
    moved = [pieces[0]]
    for piece, (up, side) in zip(pieces[1:], ((0, 1), (1, 0), (1, 1))):
        pairs = []
        for i in range(lat_count):
            for j in range(lon_count):
                to = (i + sign * up) % lat_count, (j + sign * side) % lon_count
                pairs.append((i * lon_count + j, to[0] * lon_count + to[1]))
        moved.append(lax.ppermute(piece, BOTH, pairs))
    return moved


def swapped(values):
    return lax.ppermute(values, "lat", [(i, i ^ 1) for i in range(lax.axis_size("lat"))])


def summed_everywhere(partial, core):
    lat_count, lon_count = lax.axis_size("lat"), lax.axis_size("lon")
    groups = [
        [i * lon_count + j for i in range(c, lat_count, 2) for j in range(lon_count)]
        for c in range(2)
    ]
    size = len(groups[0])
    shape = (size, partial.shape[0] // size, partial.shape[1])
    parts = lax.all_to_all(
        partial.reshape(shape), BOTH, 0, 0, tiled=True, axis_index_groups=groups
    )
    total = jnp.sum(parts.astype(F32), axis=0).astype(BF)
    half = lax.all_to_all(
        jnp.broadcast_to(total[None], shape), BOTH, 0, 0, tiled=True, axis_index_groups=groups
    ).reshape(partial.shape)
    other = swapped(half)
    first = core == 0
    return jnp.concatenate(
        [jnp.where(first, half, other), jnp.where(first, other, half)], axis=0
    ).astype(F32)


def per_device(
    tokens, fine_qkv, fine_proj, fine_up, fine_down, merge_weight, coarse_qkv, coarse_proj, cotangent
):
    shape = jax.ShapeDtypeStruct
    core = lax.axis_index("lat") % 2
    core_word = core.astype(jnp.int32).reshape(1)
    edge = jnp.where(lax.axis_index("lat") == 0, F32(-1e30), F32(0.0)).reshape(1)
    cot = cotangent.reshape(WIN, COARSE)
    cot_own = cot.astype(BF)
    cot_other = swapped(cot_own)

    cells = tokens.reshape(CELLS, FINE)
    pieces = call(
        pack, "pack_tokens", (cells, jnp.asarray(GATHER_PIECES)), piece_shapes(),
        flops=2 * PACKED * CELLS * FINE,
    )
    moved = shifted(pieces, 1)
    results = call(
        fine_forward,
        "fine_forward",
        (edge, *moved, jnp.asarray(WINDOW_FROM_PIECES), jnp.asarray(PIECES_FROM_WINDOW),
         fine_qkv, fine_proj, fine_up, fine_down),
        piece_shapes() + [
            shape((CELLS, FINE), BF), shape((CELLS, 3 * FINE), BF), shape((8, 4 * WIN, WIN), BF),
            shape((CELLS, FINE), F32), shape((CELLS, HIDDEN), BF),
        ],
        scratch=[pltpu.VMEM((CELLS, FINE), BF)],
        flops=6 * 10**9,
        scalars=1,
    )
    pieces, (x, qkv, a, att, slope) = results[:4], results[4:]
    moved = shifted(pieces, -1)
    coarse_out, fine, merged, c_qkv, c_a, own_half, sent_half = call(
        coarse_forward,
        "coarse_forward",
        (core_word, *moved, jnp.asarray(PARITY_FROM_PIECES), merge_weight, coarse_qkv, coarse_proj),
        [
            shape((WIN, COARSE), BF), shape((CELLS, FINE), BF), shape((WIN, COARSE), BF),
            shape((WIN, 3 * COARSE), BF), shape((4, 4 * WIN, WIN), BF),
            shape((WIN, COARSE // 2), BF), shape((WIN, COARSE // 2), BF),
        ],
        scratch=[pltpu.VMEM((WIN, COARSE), BF)],
        flops=2 * 10**9,
        scalars=1,
    )
    other_half = swapped(sent_half)
    partial = call(
        proj_partial,
        "proj_partial",
        (own_half, other_half, cot_own, cot_other),
        shape((COARSE // 2, COARSE), BF),
        flops=3 * 10**8,
    )
    proj_grad = summed_everywhere(partial, core)

    pieces = call(
        coarse_backward,
        "coarse_backward",
        (cot, fine, merged, c_qkv, c_a, jnp.asarray(PIECES_FROM_PARITY),
         merge_weight, coarse_qkv, coarse_proj),
        piece_shapes(),
        scratch=[pltpu.VMEM((WIN, 3 * COARSE), BF)],
        flops=2 * 10**9,
    )
    moved = shifted(pieces, 1)
    pieces = call(
        fine_backward,
        "fine_backward",
        (*moved, jnp.asarray(WINDOW_FROM_PIECES), jnp.asarray(PIECES_FROM_WINDOW),
         x, qkv, a, att, slope, fine_qkv, fine_proj, fine_up, fine_down),
        piece_shapes(),
        scratch=[pltpu.VMEM((CELLS, 3 * FINE), BF)],
        flops=6 * 10**9,
    )
    moved = shifted(pieces, -1)
    input_grad = call(
        unpack, "unpack_grad", (*moved, jnp.asarray(CELLS_FROM_PIECES)),
        shape((CELLS, FINE), F32), flops=2 * PACKED * CELLS * FINE,
    )
    return (
        coarse_out.reshape(6, 12, 2, COARSE),
        input_grad.reshape(ROWS, COLS, 2, FINE),
        proj_grad,
    )


def solution(mesh):
    field = P("lat", "lon", None, None)
    return jax.shard_map(
        per_device,
        mesh=mesh,
        in_specs=(field, P(), P(), P(), P(), P(), P(), P(), field),
        out_specs=(field, field, P()),
        check_vma=False,
    )
```

```python
import jax
import jax.numpy as jnp
import numpy as np
from jax import lax
from jax.experimental import pallas as pl
from jax.experimental.pallas import tpu as pltpu
from jax.sharding import PartitionSpec as P

BF = jnp.bfloat16
F32 = jnp.float32
ROWS = 12
COLS = 24
CELLS = ROWS * COLS * 2
WIN = 144
HALF_LAT = 3
HALF_LON = 6
FINE = 512
COARSE = 1024
HIDDEN = 2048
QUAD = 256
CHUNK = 512
PIECES = (336, 112, 112, 48)
PACKED = sum(PIECES)
EPS = 1e-05
BOTH = ("lat", "lon")


def cell_orders():
    number = np.arange(CELLS).reshape(ROWS, COLS, 2)
    r, c = ROWS - HALF_LAT, COLS - HALF_LON
    parts = (number[:r, :c], number[:r, c:], number[r:, :c], number[r:, c:])
    pieces = np.full(PACKED, -1)
    start = 0
    for part, room in zip(parts, PIECES):
        pieces[start : start + part.size] = part.reshape(-1)
        start += room
    parity = number.reshape(6, 2, 12, 2, 2).transpose(1, 3, 0, 2, 4).reshape(-1)
    place = np.zeros(CELLS, int)
    place[pieces[pieces >= 0]] = np.nonzero(pieces >= 0)[0]
    place = place.reshape(ROWS, COLS, 2)
    rolled = np.roll(place, (HALF_LAT, HALF_LON), (0, 1))
    window = rolled.reshape(2, 6, 2, 12, 2).transpose(0, 2, 1, 3, 4).reshape(-1)
    return pieces, parity, window


def selector(sources, width):
    matrix = np.zeros((len(sources), width), np.float32)
    for row, source in enumerate(sources):
        if source >= 0:
            matrix[row, source] = 1.0
    return matrix.astype(jnp.bfloat16)


PIECE_CELLS, PARITY_CELLS, WINDOW_PLACES = cell_orders()
PLACE_OF = np.zeros(CELLS, int)
PLACE_OF[PIECE_CELLS[PIECE_CELLS >= 0]] = np.nonzero(PIECE_CELLS >= 0)[0]
GATHER_PIECES = selector(PIECE_CELLS, CELLS)
WINDOW_FROM_PIECES = selector(WINDOW_PLACES, PACKED)
PIECES_FROM_WINDOW = np.ascontiguousarray(WINDOW_FROM_PIECES.T)
PARITY_FROM_PIECES = selector(PLACE_OF[PARITY_CELLS], PACKED)
PIECES_FROM_PARITY = np.ascontiguousarray(PARITY_FROM_PIECES.T)
CELLS_FROM_PIECES = selector(PLACE_OF, PACKED)


def mm(a, b):
    return jnp.dot(a, b, preferred_element_type=F32)


def mm_nt(a, b):
    return lax.dot_general(a, b, (((1,), (1,)), ((), ())), preferred_element_type=F32)


def mm_tn(a, b):
    return lax.dot_general(a, b, (((0,), (0,)), ((), ())), preferred_element_type=F32)


def normed(values):
    centered = values - jnp.mean(values, axis=-1, keepdims=True)
    scale = lax.rsqrt(jnp.mean(centered * centered, axis=-1, keepdims=True) + EPS)
    return centered * scale, scale


def normed_pull(unit, scale, grad):
    low = jnp.mean(grad, axis=-1, keepdims=True)
    along = jnp.mean(grad * unit, axis=-1, keepdims=True)
    return scale * (grad - low - unit * along)


def heads_apart(values):
    head = lax.broadcasted_iota(jnp.int32, values.shape, 1) // 64
    zero = jnp.zeros_like(values)
    return jnp.concatenate([jnp.where(head == h, values, zero) for h in range(4)], axis=0)


def heads_joined(stacked):
    rows = stacked.shape[0] // 4
    head = lax.broadcasted_iota(jnp.int32, (rows, QUAD), 1) // 64
    out = stacked[:rows]
    for h in range(1, 4):
        out = jnp.where(head == h, stacked[h * rows : (h + 1) * rows], out)
    return out


def attend(q, k, v, bias):
    apart = heads_apart(q * 0.125)
    scores = mm_nt(apart, k)
    if bias is not None:
        scores = scores + bias
    weights = jnp.exp(scores - jnp.max(scores, axis=-1, keepdims=True))
    a = (weights * (1.0 / jnp.sum(weights, axis=-1, keepdims=True))).astype(BF)
    return a, heads_joined(mm(a, v)).astype(BF)


def attend_pull(q, k, v, a, grad):
    apart = heads_apart(grad)
    af = a.astype(F32)
    weighted = mm_nt(apart, v) * af
    ds = (weighted - af * jnp.sum(weighted, axis=-1, keepdims=True)).astype(BF)
    dq = heads_joined(mm(ds, k)) * 0.125
    dk = mm_tn(ds, heads_apart(q * 0.125))
    dv = mm_tn(a, apart)
    return dq.astype(BF), dk.astype(BF), dv.astype(BF)


def gelu_pair(h):
    cdf = 0.5 * (1.0 + lax.erf(h * 0.7071067811865476))
    return h * cdf, cdf + h * (0.3989422804014327 * jnp.exp(-0.5 * h * h))


def split_pieces(packed, refs):
    start = 0
    for ref, room in zip(refs, PIECES):
        ref[...] = packed[start : start + room].astype(ref.dtype)
        start += room


def joined_pieces(refs):
    return jnp.concatenate([ref[...] for ref in refs], axis=0)


def fine_forward(
    edge, keep, beside, above, corner, order, back, qkv_w, proj_w, up_w, down_w,
    out0, out1, out2, out3, x_out, qkv_out, a_out, att_out, slope_out, mixed
):
    x = mm(order[...], joined_pieces((keep, beside, above, corner)))
    x_out[...] = x.astype(BF)
    unit, _ = normed(x)
    qkv_out[...] = mm(unit.astype(BF), qkv_w[...]).astype(BF)
    half_q = (lax.broadcasted_iota(jnp.int32, (4 * WIN, WIN), 0) % WIN) >= WIN // 2
    half_k = lax.broadcasted_iota(jnp.int32, (4 * WIN, WIN), 1) >= WIN // 2
    bias = jnp.where(half_q != half_k, edge[0], 0.0)
    for w in range(4):
        for g in range(2):
            rows, cols = slice(w * WIN, (w + 1) * WIN), g * QUAD
            a, o = attend(
                qkv_out[rows, cols : cols + QUAD],
                qkv_out[rows, FINE + cols : FINE + cols + QUAD],
                qkv_out[rows, 2 * FINE + cols : 2 * FINE + cols + QUAD],
                bias if w < 2 else None,
            )
            a_out[2 * w + g] = a
            mixed[rows, cols : cols + QUAD] = o
    attended = x + mm(mixed[...], proj_w[...])
    att_out[...] = attended
    unit, _ = normed(attended)
    unit = unit.astype(BF)
    total = attended
    for c in range(0, HIDDEN, CHUNK):
        value, slope = gelu_pair(mm(unit, up_w[:, c : c + CHUNK]))
        slope_out[:, c : c + CHUNK] = slope.astype(BF)
        total = total + mm(value.astype(BF), down_w[c : c + CHUNK])
    split_pieces(mm(back[...], total.astype(BF)), (out0, out1, out2, out3))


def coarse_forward(
    core, keep, beside, above, corner, order, merge_w, qkv_w, proj_w,
    out, fine_out, merged_out, qkv_out, a_out, own_half, sent_half, mixed
):
    fine = mm(order[...], joined_pieces((keep, beside, above, corner)))
    fine_out[...] = fine.astype(BF)
    parts = [fine[p * WIN : (p + 1) * WIN] for p in range(4)]
    mean = sum(jnp.sum(part, axis=-1, keepdims=True) for part in parts) / (4 * FINE)
    parts = [part - mean for part in parts]
    spread = sum(jnp.sum(part * part, axis=-1, keepdims=True) for part in parts) / (4 * FINE)
    scale = lax.rsqrt(spread + EPS)
    merged = jnp.zeros((WIN, COARSE), F32)
    for p in range(4):
        merged = merged + mm((parts[p] * scale).astype(BF), merge_w[p * FINE : (p + 1) * FINE])
    merged = merged.astype(BF)
    merged_out[...] = merged
    merged = merged.astype(F32)
    unit, _ = normed(merged)
    qkv_out[...] = mm(unit.astype(BF), qkv_w[...]).astype(BF)
    for g in range(4):
        cols = g * QUAD
        a, o = attend(
            qkv_out[:, cols : cols + QUAD],
            qkv_out[:, COARSE + cols : COARSE + cols + QUAD],
            qkv_out[:, 2 * COARSE + cols : 2 * COARSE + cols + QUAD],
            None,
        )
        a_out[g] = a
        mixed[:, cols : cols + QUAD] = o
    low, high = mixed[:, : COARSE // 2], mixed[:, COARSE // 2 :]
    first = core[0] == 0
    own_half[...] = jnp.where(first, low, high)
    sent_half[...] = jnp.where(first, high, low)
    out[...] = (merged + mm(mixed[...], proj_w[...])).astype(BF)


def proj_partial(own, other, cot_own, cot_other, out):
    total = mm_tn(own[...], cot_own[...].astype(BF)) + mm_tn(other[...], cot_other[...].astype(BF))
    out[...] = (total * 18432.0 ** (-0.5)).astype(BF)


def coarse_backward(
    cot, fine, merged, qkv, a, order, merge_w, qkv_w, proj_w,
    out0, out1, out2, out3, dqkv
):
    grad = mm_nt(cot[...].astype(BF), proj_w[...]).astype(BF)
    for g in range(4):
        cols = g * QUAD
        pulled = attend_pull(
            qkv[:, cols : cols + QUAD],
            qkv[:, COARSE + cols : COARSE + cols + QUAD],
            qkv[:, 2 * COARSE + cols : 2 * COARSE + cols + QUAD],
            a[g],
            grad[:, cols : cols + QUAD],
        )
        for i in range(3):
            dqkv[:, i * COARSE + cols : i * COARSE + cols + QUAD] = pulled[i]
    dn = mm_nt(dqkv[...], qkv_w[...]).astype(BF).astype(F32)
    unit, scale = normed(merged[...].astype(F32))
    merged_grad = (cot[...] + normed_pull(unit, scale, dn)).astype(BF)
    parts = [fine[p * WIN : (p + 1) * WIN].astype(F32) for p in range(4)]
    mean = sum(jnp.sum(part, axis=-1, keepdims=True) for part in parts) / (4 * FINE)
    parts = [part - mean for part in parts]
    spread = sum(jnp.sum(part * part, axis=-1, keepdims=True) for part in parts) / (4 * FINE)
    scale = lax.rsqrt(spread + EPS)
    units = [part * scale for part in parts]
    grads = [
        mm_nt(merged_grad, merge_w[p * FINE : (p + 1) * FINE]).astype(BF).astype(F32)
        for p in range(4)
    ]
    low = sum(jnp.sum(g, axis=-1, keepdims=True) for g in grads) / (4 * FINE)
    along = sum(jnp.sum(g * u, axis=-1, keepdims=True) for g, u in zip(grads, units)) / (4 * FINE)
    fine_grad = jnp.concatenate(
        [(scale * (g - low - u * along)).astype(BF) for g, u in zip(grads, units)], axis=0
    )
    split_pieces(mm(order[...], fine_grad), (out0, out1, out2, out3))


def fine_backward(
    keep, beside, above, corner, order, back, x, qkv, a, att, slope, qkv_w, proj_w, up_w, down_w,
    out0, out1, out2, out3, dqkv
):
    incoming = mm(order[...], joined_pieces((keep, beside, above, corner)))
    rounded = incoming.astype(BF)
    dn = jnp.zeros((CELLS, FINE), F32)
    for c in range(0, HIDDEN, CHUNK):
        dh = mm_nt(rounded, down_w[c : c + CHUNK]) * slope[:, c : c + CHUNK].astype(F32)
        dn = dn + mm_nt(dh.astype(BF), up_w[:, c : c + CHUNK])
    unit, scale = normed(att[...])
    att_grad = incoming + normed_pull(unit, scale, dn)
    grad = mm_nt(att_grad.astype(BF), proj_w[...]).astype(BF)
    for w in range(4):
        for g in range(2):
            rows, cols = slice(w * WIN, (w + 1) * WIN), g * QUAD
            pulled = attend_pull(
                qkv[rows, cols : cols + QUAD],
                qkv[rows, FINE + cols : FINE + cols + QUAD],
                qkv[rows, 2 * FINE + cols : 2 * FINE + cols + QUAD],
                a[2 * w + g],
                grad[rows, cols : cols + QUAD],
            )
            for i in range(3):
                dqkv[rows, i * FINE + cols : i * FINE + cols + QUAD] = pulled[i]
    dn = mm_nt(dqkv[...], qkv_w[...])
    unit, scale = normed(x[...].astype(F32))
    total = att_grad + normed_pull(unit, scale, dn)
    split_pieces(mm(back[...], total.astype(BF)), (out0, out1, out2, out3))


def unpack(keep, beside, above, corner, order, out):
    out[...] = mm(order[...], joined_pieces((keep, beside, above, corner)))


def pack(cells, order, out0, out1, out2, out3):
    split_pieces(mm(order[...], cells[...]), (out0, out1, out2, out3))


def share_sum(parts, after, out):
    total = parts[0].astype(F32)
    for i in range(1, parts.shape[0]):
        total = total + parts[i].astype(F32)
    total = total.astype(BF)
    for i in range(parts.shape[0]):
        out[i] = total


def join_halves(core, half, other, after, out):
    first = core[0] == 0
    rows = COARSE // 2
    low = jnp.where(first, half[...], other[...])
    high = jnp.where(first, other[...], half[...])
    out[:rows] = low.astype(F32).reshape(rows, COARSE)
    out[rows:] = high.astype(F32).reshape(rows, COARSE)


def call(body, name, operands, outs, scratch=(), micros=1, scalars=0, after=None):
    vmem = pl.BlockSpec(memory_space=pltpu.VMEM)
    smem = pl.BlockSpec(memory_space=pltpu.SMEM)
    waits = [] if after is None else [pl.BlockSpec(memory_space=pl.ANY)]
    moved = sum(int(np.prod(o.shape)) * o.dtype.itemsize for o in jax.tree.leaves((operands, outs)))
    return pl.pallas_call(
        body,
        name=name,
        out_shape=outs,
        in_specs=[smem] * scalars + [vmem] * (len(operands) - scalars) + waits,
        out_specs=jax.tree.map(lambda _: vmem, outs),
        scratch_shapes=list(scratch),
        compiler_params=pltpu.CompilerParams(vmem_limit_bytes=60 * 2**20),
        cost_estimate=pl.CostEstimate(
            flops=micros * 1153 * 10**6, bytes_accessed=moved, transcendentals=0
        ),
    )(*operands, *([] if after is None else [after]))


def piece_shapes():
    return [jax.ShapeDtypeStruct((room, FINE), BF) for room in PIECES]


def shifted(pieces, sign):
    lat_count, lon_count = lax.axis_size("lat"), lax.axis_size("lon")
    moved = [pieces[0]]
    for piece, (up, side) in zip(pieces[1:], ((0, 1), (1, 0), (1, 1))):
        pairs = []
        for i in range(lat_count):
            for j in range(lon_count):
                to = (i + sign * up) % lat_count, (j + sign * side) % lon_count
                pairs.append((i * lon_count + j, to[0] * lon_count + to[1]))
        moved.append(lax.ppermute(piece, BOTH, pairs))
    return moved


def swapped(values):
    return lax.ppermute(values, "lat", [(i, i ^ 1) for i in range(lax.axis_size("lat"))])


def same_core(values):
    lat_count, lon_count = lax.axis_size("lat"), lax.axis_size("lon")
    groups = [
        [i * lon_count + j for i in range(c, lat_count, 2) for j in range(lon_count)]
        for c in range(2)
    ]
    return lax.all_to_all(values, BOTH, 0, 0, tiled=True, axis_index_groups=groups)


def per_device(
    tokens, fine_qkv, fine_proj, fine_up, fine_down, merge_weight, coarse_qkv, coarse_proj, cotangent
):
    shape = jax.ShapeDtypeStruct
    core = lax.axis_index("lat") % 2
    core_word = core.astype(jnp.int32).reshape(1)
    edge = jnp.where(lax.axis_index("lat") == 0, F32(-1e30), F32(0.0)).reshape(1)
    cot = cotangent.reshape(WIN, COARSE)
    cot_other = swapped(cotangent).reshape(WIN, COARSE)

    cells = tokens.reshape(CELLS, FINE)
    pieces = call(
        pack, "pack_tokens", (cells, jnp.asarray(GATHER_PIECES)), piece_shapes(),
        micros=3,
    )
    moved = shifted(pieces, 1)
    results = call(
        fine_forward,
        "fine_forward",
        (edge, *moved, jnp.asarray(WINDOW_FROM_PIECES), jnp.asarray(PIECES_FROM_WINDOW),
         fine_qkv, fine_proj, fine_up, fine_down),
        piece_shapes() + [
            shape((CELLS, FINE), BF), shape((CELLS, 3 * FINE), BF), shape((8, 4 * WIN, WIN), BF),
            shape((CELLS, FINE), F32), shape((CELLS, HIDDEN), BF),
        ],
        scratch=[pltpu.VMEM((CELLS, FINE), BF)],
        micros=14,
        scalars=1,
    )
    pieces, (x, qkv, a, att, slope) = results[:4], results[4:]
    moved = shifted(pieces, -1)
    coarse_out, fine, merged, c_qkv, c_a, own_half, sent_half = call(
        coarse_forward,
        "coarse_forward",
        (core_word, *moved, jnp.asarray(PARITY_FROM_PIECES), merge_weight, coarse_qkv, coarse_proj),
        [
            shape((WIN, COARSE), BF), shape((CELLS, FINE), BF), shape((WIN, COARSE), BF),
            shape((WIN, 3 * COARSE), BF), shape((4, 4 * WIN, WIN), BF),
            shape((WIN, COARSE // 2), BF), shape((WIN, COARSE // 2), BF),
        ],
        scratch=[pltpu.VMEM((WIN, COARSE), BF)],
        micros=11,
        scalars=1,
    )
    other_half = swapped(sent_half)
    partial = call(
        proj_partial,
        "proj_partial",
        (own_half, other_half, cot, cot_other),
        shape((COARSE // 2, COARSE), BF),
        micros=3,
    )
    sharers = lax.axis_size("lat") * lax.axis_size("lon") // 2
    shares = same_core(partial.reshape(sharers, COARSE // 2 // sharers, COARSE))

    pieces = call(
        coarse_backward,
        "coarse_backward",
        (cot, fine, merged, c_qkv, c_a, jnp.asarray(PIECES_FROM_PARITY),
         merge_weight, coarse_qkv, coarse_proj),
        piece_shapes(),
        scratch=[pltpu.VMEM((WIN, 3 * COARSE), BF)],
        micros=11,
    )
    summed = call(
        share_sum, "share_sum", (shares,), shape(shares.shape, BF), micros=2, after=pieces[3]
    )
    half = same_core(summed)
    moved = shifted(pieces, 1)
    pieces = call(
        fine_backward,
        "fine_backward",
        (*moved, jnp.asarray(WINDOW_FROM_PIECES), jnp.asarray(PIECES_FROM_WINDOW),
         x, qkv, a, att, slope, fine_qkv, fine_proj, fine_up, fine_down),
        piece_shapes(),
        scratch=[pltpu.VMEM((CELLS, 3 * FINE), BF)],
        micros=14,
    )
    half, corner = lax.optimization_barrier((half, pieces[3]))
    pieces = [*pieces[:3], corner]
    other = swapped(half)
    proj_grad = call(
        join_halves, "join_halves", (core_word, half, other), shape((COARSE, COARSE), F32),
        micros=3, scalars=1, after=pieces[3],
    )
    moved = shifted(pieces, -1)
    input_grad = call(
        unpack, "unpack_grad", (*moved, jnp.asarray(CELLS_FROM_PIECES)),
        shape((CELLS, FINE), F32), micros=3,
    )
    return (
        coarse_out.reshape(6, 12, 2, COARSE),
        input_grad.reshape(ROWS, COLS, 2, FINE),
        proj_grad,
    )


def solution(mesh):
    field = P("lat", "lon", None, None)
    return jax.shard_map(
        per_device,
        mesh=mesh,
        in_specs=(field, P(), P(), P(), P(), P(), P(), P(), field),
        out_specs=(field, field, P()),
        check_vma=False,
    )
```

```python
import jax
import jax.numpy as jnp
import numpy as np
from jax import lax
from jax.experimental import pallas as pl
from jax.experimental.pallas import tpu as pltpu
from jax.sharding import PartitionSpec as P

BF = jnp.bfloat16
F32 = jnp.float32
ROWS = 12
COLS = 24
CELLS = ROWS * COLS * 2
WIN = 144
HALF_LAT = 3
HALF_LON = 6
FINE = 512
COARSE = 1024
HIDDEN = 2048
QUAD = 256
CHUNK = 512
PIECES = (336, 112, 112, 48)
PACKED = sum(PIECES)
EPS = 1e-05
BOTH = ("lat", "lon")
LIMIT = 26 * 2**20


def cell_orders():
    number = np.arange(CELLS).reshape(ROWS, COLS, 2)
    r, c = ROWS - HALF_LAT, COLS - HALF_LON
    parts = (number[:r, :c], number[:r, c:], number[r:, :c], number[r:, c:])
    pieces = np.full(PACKED, -1)
    start = 0
    for part, room in zip(parts, PIECES):
        pieces[start : start + part.size] = part.reshape(-1)
        start += room
    parity = number.reshape(6, 2, 12, 2, 2).transpose(1, 3, 0, 2, 4).reshape(-1)
    place = np.zeros(CELLS, int)
    place[pieces[pieces >= 0]] = np.nonzero(pieces >= 0)[0]
    place = place.reshape(ROWS, COLS, 2)
    rolled = np.roll(place, (HALF_LAT, HALF_LON), (0, 1))
    window = rolled.reshape(2, 6, 2, 12, 2).transpose(0, 2, 1, 3, 4).reshape(-1)
    return pieces, parity, window


PIECE_CELLS, PARITY_CELLS, WINDOW_PLACES = cell_orders()
PLACE_OF = np.zeros(CELLS, np.int32)
PLACE_OF[PIECE_CELLS[PIECE_CELLS >= 0]] = np.nonzero(PIECE_CELLS >= 0)[0]


def targets(places):
    rows = np.full(PACKED, -1, np.int32)
    rows[places] = np.arange(CELLS, dtype=np.int32)
    return rows.reshape(1, PACKED)


PLACE_OF_PARITY = PLACE_OF[PARITY_CELLS].reshape(1, CELLS)
PLACE_OF_WINDOW = WINDOW_PLACES.astype(np.int32).reshape(1, CELLS)
WINDOW_AT = targets(WINDOW_PLACES)
PARITY_AT = targets(PLACE_OF[PARITY_CELLS])
CELL_AT = targets(PLACE_OF)


def moved_rows(target, values, rows):
    row = lax.broadcasted_iota(jnp.int32, (rows, target.shape[1]), 0)
    return mm(jnp.where(row == target[...], 1.0, 0.0).astype(BF), values)


class Loads:
    def __init__(self, sems, ahead=16 * 2**20):
        self.sems, self.ahead, self.queue, self.started = sems, ahead, [], 0

    def add(self, name, source, target, *where):
        copy = pltpu.make_async_copy(
            source.at[where], target.at[where], self.sems.at[len(self.queue)]
        )
        size = int(np.prod(target.at[where].shape)) * target.dtype.itemsize
        number = len([entry for entry in self.queue if entry[0] == name])
        self.queue.append((name, number, copy, size))

    def start(self, done):
        flying = sum(entry[3] for entry in self.queue[done : self.started])
        while self.started < len(self.queue) and (
            self.started <= done or flying + self.queue[self.started][3] <= self.ahead
        ):
            flying += self.queue[self.started][3]
            self.queue[self.started][2].start()
            self.started += 1

    def wait(self, name, number=0):
        (place,) = [i for i, entry in enumerate(self.queue) if entry[:2] == (name, number)]
        self.start(place)
        self.queue[place][2].wait()
        self.start(place + 1)


class Stores:
    def __init__(self, sems):
        self.sems, self.copies = sems, []

    def start(self, source, target, *where):
        copy = pltpu.make_async_copy(
            source.at[where], target.at[where], self.sems.at[len(self.copies)]
        )
        copy.start()
        self.copies.append(copy)

    def finish(self):
        for copy in self.copies:
            copy.wait()


FULL = slice(None)


def chunk(index, size=CHUNK):
    return pl.ds(index * size, size)


def mm(a, b):
    return jnp.dot(a, b, preferred_element_type=F32)


def mm_nt(a, b):
    return lax.dot_general(a, b, (((1,), (1,)), ((), ())), preferred_element_type=F32)


def mm_tn(a, b):
    return lax.dot_general(a, b, (((0,), (0,)), ((), ())), preferred_element_type=F32)


def normed(values):
    centered = values - jnp.mean(values, axis=-1, keepdims=True)
    scale = lax.rsqrt(jnp.mean(centered * centered, axis=-1, keepdims=True) + EPS)
    return centered * scale, scale


def normed_pull(unit, scale, grad):
    low = jnp.mean(grad, axis=-1, keepdims=True)
    along = jnp.mean(grad * unit, axis=-1, keepdims=True)
    return scale * (grad - low - unit * along)


def heads_apart(values):
    head = lax.broadcasted_iota(jnp.int32, values.shape, 1) // 64
    zero = jnp.zeros_like(values)
    return jnp.concatenate([jnp.where(head == h, values, zero) for h in range(4)], axis=0)


def heads_joined(stacked):
    rows = stacked.shape[0] // 4
    head = lax.broadcasted_iota(jnp.int32, (rows, QUAD), 1) // 64
    out = stacked[:rows]
    for h in range(1, 4):
        out = jnp.where(head == h, stacked[h * rows : (h + 1) * rows], out)
    return out


def attend(q, k, v, bias):
    apart = heads_apart(q * 0.125)
    scores = mm_nt(apart, k)
    if bias is not None:
        scores = scores + bias
    weights = jnp.exp(scores - jnp.max(scores, axis=-1, keepdims=True))
    a = (weights * (1.0 / jnp.sum(weights, axis=-1, keepdims=True))).astype(BF)
    return a, heads_joined(mm(a, v)).astype(BF)


def attend_pull(q, k, v, a, grad):
    apart = heads_apart(grad)
    af = a.astype(F32)
    weighted = mm_nt(apart, v) * af
    ds = (weighted - af * jnp.sum(weighted, axis=-1, keepdims=True)).astype(BF)
    dq = heads_joined(mm(ds, k)) * 0.125
    dk = mm_tn(ds, heads_apart(q * 0.125))
    dv = mm_tn(a, apart)
    return dq.astype(BF), dk.astype(BF), dv.astype(BF)


def gelu_pair(h):
    cdf = 0.5 * (1.0 + lax.erf(h * 0.7071067811865476))
    return h * cdf, cdf + h * (0.3989422804014327 * jnp.exp(-0.5 * h * h))


def split_pieces(packed, refs):
    start = 0
    for ref, room in zip(refs, PIECES):
        ref[...] = packed[start : start + room].astype(ref.dtype)
        start += room


def joined_pieces(refs):
    return jnp.concatenate([ref[...] for ref in refs], axis=0)


def fine_forward(
    keep, beside, above, corner, window_at, place_of_window, qkv_w, proj_w, up_w, down_w,
    out0, out1, out2, out3, x_hbm, qkv_hbm, a_hbm, att_hbm, slope_hbm,
    x_out, qkv_out, a_out, att_out, slope_out, mixed, sems
):
    stores = Stores(sems)
    x = moved_rows(window_at, joined_pieces((keep, beside, above, corner)), CELLS)
    x_out[...] = x.astype(BF)
    stores.start(x_out, x_hbm)
    unit, _ = normed(x)
    unit = unit.astype(BF)
    for i in range(3):
        qkv_out[:, chunk(i)] = mm(unit, qkv_w[:, chunk(i)]).astype(BF)
    stores.start(qkv_out, qkv_hbm)
    half_q = (lax.broadcasted_iota(jnp.int32, (4 * WIN, WIN), 0) % WIN) >= WIN // 2
    half_k = lax.broadcasted_iota(jnp.int32, (4 * WIN, WIN), 1) >= WIN // 2
    apart = jnp.where(lax.axis_index("lat") == 0, -1e30, 0.0)
    bias = jnp.where(half_q != half_k, apart, 0.0)
    for w in range(4):
        for g in range(2):
            rows, cols = slice(w * WIN, (w + 1) * WIN), g * QUAD
            a, o = attend(
                qkv_out[rows, cols : cols + QUAD],
                qkv_out[rows, FINE + cols : FINE + cols + QUAD],
                qkv_out[rows, 2 * FINE + cols : 2 * FINE + cols + QUAD],
                bias if w < 2 else None,
            )
            a_out[2 * w + g] = a
            mixed[rows, cols : cols + QUAD] = o
        stores.start(a_out, a_hbm, pl.ds(2 * w, 2))
    attended = x + mm(mixed[...], proj_w[...])
    att_out[...] = attended
    stores.start(att_out, att_hbm)
    unit, _ = normed(attended)
    unit = unit.astype(BF)
    total = attended
    for c in range(HIDDEN // CHUNK):
        value, slope = gelu_pair(mm(unit, up_w[:, chunk(c)]))
        slope_out[:, chunk(c)] = slope.astype(BF)
        stores.start(slope_out, slope_hbm, FULL, chunk(c))
        total = total + mm(value.astype(BF), down_w[chunk(c)])
    split_pieces(
        moved_rows(place_of_window, total.astype(BF), PACKED), (out0, out1, out2, out3)
    )
    stores.finish()


def merge_unit(parts):
    mean = sum(jnp.sum(part, axis=-1, keepdims=True) for part in parts) / (4 * FINE)
    parts = [part - mean for part in parts]
    spread = sum(jnp.sum(part * part, axis=-1, keepdims=True) for part in parts) / (4 * FINE)
    scale = lax.rsqrt(spread + EPS)
    return [part * scale for part in parts], scale


def coarse_forward(
    keep, beside, above, corner, parity_at, merge_w, qkv_w, cot_in,
    own_half, sent_half, fine_hbm, merged_hbm, qkv_hbm, a_hbm, o_hbm,
    fine_out, merged_out, qkv_out, a_out, mixed, sems
):
    stores = Stores(sems)
    fine = moved_rows(parity_at, joined_pieces((keep, beside, above, corner)), CELLS)
    fine_out[...] = fine.astype(BF)
    stores.start(fine_out, fine_hbm)
    units, _ = merge_unit([fine[p * WIN : (p + 1) * WIN] for p in range(4)])
    merged = jnp.zeros((WIN, COARSE), F32)
    for p in range(4):
        merged = merged + mm(units[p].astype(BF), merge_w[chunk(p)])
    merged = merged.astype(BF)
    merged_out[...] = merged
    stores.start(merged_out, merged_hbm)
    unit, _ = normed(merged.astype(F32))
    unit = unit.astype(BF)
    for i in range(3):
        qkv_out[:, chunk(i, COARSE)] = mm(unit, qkv_w[:, chunk(i, COARSE)]).astype(BF)
    stores.start(qkv_out, qkv_hbm)
    cot = cot_in[...].reshape(WIN, COARSE).astype(BF)
    for g in range(4):
        cols = g * QUAD
        a, o = attend(
            qkv_out[:, cols : cols + QUAD],
            qkv_out[:, COARSE + cols : COARSE + cols + QUAD],
            qkv_out[:, 2 * COARSE + cols : 2 * COARSE + cols + QUAD],
            None,
        )
        a_out[g] = a
        mixed[:, cols : cols + QUAD] = o
        stores.start(a_out, a_hbm, pl.ds(g, 1))
    stores.start(mixed, o_hbm)
    first = lax.axis_index("lat") % 2 == 0
    low = mm_tn(mixed[:, : COARSE // 2], cot) * 18432.0 ** (-0.5)
    high = mm_tn(mixed[:, COARSE // 2 :], cot) * 18432.0 ** (-0.5)
    own_half[...] = jnp.where(first, low, high).astype(BF)
    sent_half[...] = jnp.where(first, high, low).astype(BF)
    stores.finish()


def coarse_backward(
    place_of_parity, cot_hbm, proj_hbm, qkv_res, a_hbm, qkv_hbm, merged_hbm, fine_hbm, merge_hbm, o_hbm,
    out0, out1, out2, out3, out_hbm,
    cot_in, proj_w, qkv, a, qkv_w, merged, fine, merge_w, o, coarse_out, dqkv, in_sems, out_sems
):
    loads, stores = Loads(in_sems), Stores(out_sems)
    loads.add("cot", cot_hbm, cot_in)
    for i in range(2):
        loads.add("proj", proj_hbm, proj_w, chunk(i))
    loads.add("qkv", qkv_res, qkv)
    for g in range(4):
        loads.add("a", a_hbm, a, pl.ds(g, 1))
    loads.add("merged", merged_hbm, merged)
    loads.add("o", o_hbm, o)
    for i in range(3):
        loads.add("qkv_w", qkv_hbm, qkv_w, FULL, chunk(i, COARSE))
    loads.add("fine", fine_hbm, fine)
    for p in range(4):
        loads.add("merge", merge_hbm, merge_w, chunk(p))
    loads.start(0)
    loads.wait("cot")
    cot = cot_in[...].reshape(WIN, COARSE)
    cot_b = cot.astype(BF)
    grads = []
    for i in range(2):
        loads.wait("proj", i)
        grads.append(mm_nt(cot_b, proj_w[chunk(i)]).astype(BF))
    grad = jnp.concatenate(grads, axis=1)
    loads.wait("qkv")
    for g in range(4):
        loads.wait("a", g)
        cols = g * QUAD
        pulled = attend_pull(
            qkv[:, cols : cols + QUAD],
            qkv[:, COARSE + cols : COARSE + cols + QUAD],
            qkv[:, 2 * COARSE + cols : 2 * COARSE + cols + QUAD],
            a[g],
            grad[:, cols : cols + QUAD],
        )
        for i in range(3):
            dqkv[:, i * COARSE + cols : i * COARSE + cols + QUAD] = pulled[i]
    loads.wait("merged")
    loads.wait("o")
    merged_f = merged[...].astype(F32)
    full = (merged_f + mm(o[...], proj_w[...])).astype(BF)
    coarse_out[...] = full.astype(F32).reshape(coarse_out.shape).astype(BF)
    stores.start(coarse_out, out_hbm)
    dn = jnp.zeros((WIN, COARSE), F32)
    for i in range(3):
        loads.wait("qkv_w", i)
        dn = dn + mm_nt(dqkv[:, chunk(i, COARSE)], qkv_w[:, chunk(i, COARSE)])
    dn = dn.astype(BF).astype(F32)
    unit, scale = normed(merged_f)
    merged_grad = (cot + normed_pull(unit, scale, dn)).astype(BF)
    loads.wait("fine")
    units, scale = merge_unit([fine[p * WIN : (p + 1) * WIN].astype(F32) for p in range(4)])
    grads = []
    for p in range(4):
        loads.wait("merge", p)
        grads.append(mm_nt(merged_grad, merge_w[chunk(p)]).astype(BF).astype(F32))
    low = sum(jnp.sum(g, axis=-1, keepdims=True) for g in grads) / (4 * FINE)
    along = sum(jnp.sum(g * u, axis=-1, keepdims=True) for g, u in zip(grads, units)) / (4 * FINE)
    fine_grad = jnp.concatenate(
        [(scale * (g - low - u * along)).astype(BF) for g, u in zip(grads, units)], axis=0
    )
    split_pieces(moved_rows(place_of_parity, fine_grad, PACKED), (out0, out1, out2, out3))
    stores.finish()


def fine_backward(
    keep, beside, above, corner, window_at, place_of_window,
    x_hbm, qkv_res, a_hbm, att_hbm, slope_hbm, qkv_hbm, proj_hbm, up_hbm, down_hbm,
    out0, out1, out2, out3,
    x, qkv, a, att, slope, qkv_w, proj_w, up_w, down_w, dqkv, in_sems
):
    loads = Loads(in_sems)
    for c in range(HIDDEN // CHUNK):
        loads.add("down", down_hbm, down_w, chunk(c))
        loads.add("slope", slope_hbm, slope, FULL, chunk(c))
        loads.add("up", up_hbm, up_w, FULL, chunk(c))
    loads.add("att", att_hbm, att)
    loads.add("proj", proj_hbm, proj_w)
    loads.add("qkv", qkv_res, qkv)
    for w in range(4):
        loads.add("a", a_hbm, a, pl.ds(2 * w, 2))
    for i in range(3):
        loads.add("qkv_w", qkv_hbm, qkv_w, FULL, chunk(i))
    loads.add("x", x_hbm, x)
    loads.start(0)
    incoming = moved_rows(window_at, joined_pieces((keep, beside, above, corner)), CELLS)
    rounded = incoming.astype(BF)
    dn = jnp.zeros((CELLS, FINE), F32)
    for c in range(HIDDEN // CHUNK):
        loads.wait("down", c)
        loads.wait("slope", c)
        dh = mm_nt(rounded, down_w[chunk(c)]) * slope[:, chunk(c)].astype(F32)
        loads.wait("up", c)
        dn = dn + mm_nt(dh.astype(BF), up_w[:, chunk(c)])
    loads.wait("att")
    unit, scale = normed(att[...])
    att_grad = incoming + normed_pull(unit, scale, dn)
    loads.wait("proj")
    grad = mm_nt(att_grad.astype(BF), proj_w[...]).astype(BF)
    loads.wait("qkv")
    for w in range(4):
        loads.wait("a", w)
        for g in range(2):
            rows, cols = slice(w * WIN, (w + 1) * WIN), g * QUAD
            pulled = attend_pull(
                qkv[rows, cols : cols + QUAD],
                qkv[rows, FINE + cols : FINE + cols + QUAD],
                qkv[rows, 2 * FINE + cols : 2 * FINE + cols + QUAD],
                a[2 * w + g],
                grad[rows, cols : cols + QUAD],
            )
            for i in range(3):
                dqkv[rows, i * FINE + cols : i * FINE + cols + QUAD] = pulled[i]
    dn = jnp.zeros((CELLS, FINE), F32)
    for i in range(3):
        loads.wait("qkv_w", i)
        dn = dn + mm_nt(dqkv[:, chunk(i)], qkv_w[:, chunk(i)])
    loads.wait("x")
    unit, scale = normed(x[...].astype(F32))
    total = att_grad + normed_pull(unit, scale, dn)
    split_pieces(
        moved_rows(place_of_window, total.astype(BF), PACKED), (out0, out1, out2, out3)
    )


def pack(cells, out0, out1, out2, out3):
    cell = lax.broadcasted_iota(jnp.int32, (1, CELLS), 1)
    line, kept = 2 * COLS, 2 * (COLS - HALF_LON)
    row = sum((cell >= line * r).astype(jnp.int32) for r in range(1, ROWS))
    across = cell - line * row
    rest, side = row - (ROWS - HALF_LAT), across - kept
    starts = [sum(PIECES[:i]) for i in range(4)]
    inner = jnp.where(side < 0, row * kept + across, starts[1] + row * (line - kept) + side)
    outer = jnp.where(
        side < 0, starts[2] + rest * kept + across, starts[3] + rest * (line - kept) + side
    )
    place = jnp.where(rest < 0, inner, outer)
    flat = cells[...].reshape(CELLS, FINE)
    split_pieces(moved_rows(place, flat, PACKED), (out0, out1, out2, out3))


def fetch(*refs):
    count = (len(refs) - 1) // 2
    copies = [
        pltpu.make_async_copy(refs[i], refs[count + i], refs[-1].at[i]) for i in range(count)
    ]
    for copy in copies:
        copy.start()
    for copy in copies:
        copy.wait()


def unpack(keep, beside, above, corner, cell_at, out_hbm, out, sems):
    stores = Stores(sems)
    pieces = joined_pieces((keep, beside, above, corner))
    cells = moved_rows(cell_at, pieces, CELLS)
    part = ROWS // 3
    for i in range(3):
        rows = cells[i * CELLS // 3 : (i + 1) * CELLS // 3]
        out[pl.ds(i * part, part)] = rows.reshape(part, COLS, 2, FINE)
        stores.start(out, out_hbm, pl.ds(i * part, part))
    stores.finish()


def pair_sum(own, other, out):
    out[...] = (own[...].astype(F32) + other[...].astype(F32)).astype(BF)


def share_sum(parts, after, out):
    total = parts[0].astype(F32)
    for i in range(1, parts.shape[0]):
        total = total + parts[i].astype(F32)
    total = total.astype(BF)
    for i in range(parts.shape[0]):
        out[i] = total


def write_half(half, rows, out_hbm, wide, sems):
    stores = Stores(sems)
    part = COARSE // 8
    for i in range(4):
        wide[pl.ds(i * part, part)] = half[pl.ds(i * part, part)].astype(F32)
        copy = pltpu.make_async_copy(
            wide.at[pl.ds(i * part, part)],
            out_hbm.at[pl.ds(pl.multiple_of(rows + i * part, part), part)],
            sems.at[i],
        )
        copy.start()
        stores.copies.append(copy)
    stores.finish()


def first_half(half, out_hbm, wide, sems):
    write_half(half, (lax.axis_index("lat") % 2) * (COARSE // 2), out_hbm, wide, sems)


def second_half(half, begun, out_hbm, wide, sems):
    write_half(half, (1 - lax.axis_index("lat") % 2) * (COARSE // 2), out_hbm, wide, sems)


def compiler_params():
    return pltpu.CompilerParams(vmem_limit_bytes=LIMIT)


def cost(micros, operands, outs):
    moved = sum(int(np.prod(o.shape)) * o.dtype.itemsize for o in jax.tree.leaves((operands, outs)))
    return pl.CostEstimate(
        flops=micros * 1153 * 10**6, bytes_accessed=moved, transcendentals=0
    )


def call(body, name, smem=(), vmem=(), hbm=(), outs=(), hbm_outs=(), scratch=(), sems=(), micros=1, after=()):
    hbm = [pltpu.with_memory_space_constraint(o, pltpu.HBM) for o in hbm]
    operands = [*smem, *vmem, *hbm]
    staged = [pltpu.VMEM(o.shape, o.dtype) for o in [*hbm, *hbm_outs]]
    waits = list(after)
    spaces = [pltpu.SMEM] * len(smem) + [pltpu.VMEM] * len(vmem) + [pltpu.HBM] * len(hbm)
    spaces += [pl.ANY] * len(waits)
    results = [pltpu.VMEM] * len(outs) + [pltpu.HBM] * len(hbm_outs)
    return pl.pallas_call(
        body,
        name=name,
        out_shape=[
            *[pltpu.VMEM(o.shape, o.dtype) for o in outs], *[pltpu.HBM(o.shape, o.dtype) for o in hbm_outs]
        ],
        in_specs=[pl.BlockSpec(memory_space=space) for space in spaces],
        out_specs=[pl.BlockSpec(memory_space=space) for space in results],
        scratch_shapes=[*staged, *scratch] + ([pltpu.SemaphoreType.DMA((n,)) for n in sems]),
        compiler_params=compiler_params(),
        cost_estimate=cost(micros, operands, [*outs, *hbm_outs]),
    )(*operands, *waits)


def fetched(name, arrays, after=None, micros=2):
    hbm = [pltpu.with_memory_space_constraint(array, pltpu.HBM) for array in arrays]
    spec = [pl.BlockSpec(memory_space=pltpu.HBM)] * len(hbm)
    waits = [] if after is None else [after]

    def body(*refs):
        fetch(*refs[: len(hbm)], *refs[len(hbm) + len(waits) :])

    return pl.pallas_call(
        body,
        name=name,
        out_shape=[pltpu.VMEM(array.shape, array.dtype) for array in arrays],
        in_specs=spec + [pl.BlockSpec(memory_space=pl.ANY)] * len(waits),
        out_specs=[pl.BlockSpec(memory_space=pltpu.VMEM)] * len(hbm),
        scratch_shapes=[pltpu.SemaphoreType.DMA((len(hbm),))],
        compiler_params=compiler_params(),
        cost_estimate=cost(micros, arrays, arrays),
    )(*hbm, *waits)


def half_written(half, begun=None):
    half = half.reshape(COARSE // 2, COARSE)
    hbm = pl.BlockSpec(memory_space=pltpu.HBM)
    last = begun is not None
    return pl.pallas_call(
        second_half if last else first_half,
        name="second_half" if last else "first_half",
        out_shape=pltpu.HBM((COARSE, COARSE), F32),
        in_specs=[pl.BlockSpec(memory_space=pltpu.VMEM)] + [hbm] * last,
        out_specs=hbm,
        input_output_aliases={1: 0} if last else {},
        scratch_shapes=[pltpu.VMEM((COARSE // 2, COARSE), F32), pltpu.SemaphoreType.DMA((4,))],
        compiler_params=compiler_params(),
        cost_estimate=cost(2, half, half),
    )(half, *([begun] if last else []))


def piece_shapes():
    return [jax.ShapeDtypeStruct((room, FINE), BF) for room in PIECES]


def shifted(pieces, sign):
    lat_count, lon_count = lax.axis_size("lat"), lax.axis_size("lon")
    moved = [pieces[0]]
    for piece, (up, side) in zip(pieces[1:], ((0, 1), (1, 0), (1, 1))):
        pairs = []
        for i in range(lat_count):
            for j in range(lon_count):
                to = (i + sign * up) % lat_count, (j + sign * side) % lon_count
                pairs.append((i * lon_count + j, to[0] * lon_count + to[1]))
        moved.append(lax.ppermute(piece, BOTH, pairs))
    return moved


def swapped(values):
    return lax.ppermute(values, "lat", [(i, i ^ 1) for i in range(lax.axis_size("lat"))])


def same_core(values):
    lat_count, lon_count = lax.axis_size("lat"), lax.axis_size("lon")
    groups = [
        [i * lon_count + j for i in range(c, lat_count, 2) for j in range(lon_count)]
        for c in range(2)
    ]
    return lax.all_to_all(values, BOTH, 0, 0, tiled=True, axis_index_groups=groups)


def per_device(
    tokens, fine_qkv, fine_proj, fine_up, fine_down, merge_weight, coarse_qkv, coarse_proj, cotangent
):
    shape = jax.ShapeDtypeStruct
    pieces = call(
        pack, "pack_tokens", vmem=(tokens,),
        outs=piece_shapes(), micros=2,
    )
    fine_weights = fetched(
        "fetch_fine", (fine_qkv, fine_proj, fine_up, fine_down), after=pieces[3]
    )
    moved = shifted(pieces, 1)
    results = call(
        fine_forward,
        "fine_forward",
        vmem=(*moved, jnp.asarray(WINDOW_AT), jnp.asarray(PLACE_OF_WINDOW), *fine_weights),
        outs=piece_shapes(),
        hbm_outs=[
            shape((CELLS, FINE), BF), shape((CELLS, 3 * FINE), BF), shape((8, 4 * WIN, WIN), BF),
            shape((CELLS, FINE), F32), shape((CELLS, HIDDEN), BF),
        ],
        scratch=[pltpu.VMEM((CELLS, FINE), BF)],
        sems=(11,),
        micros=9,
    )
    pieces, saved = results[:4], results[4:]
    coarse_weights = fetched(
        "fetch_coarse", (merge_weight, coarse_qkv, cotangent), after=pieces[3], micros=5
    )
    moved = shifted(pieces, -1)
    own_half, sent_half, fine, merged, c_qkv, c_a, c_o = call(
        coarse_forward,
        "coarse_forward",
        vmem=(*moved, jnp.asarray(PARITY_AT), *coarse_weights),
        outs=[shape((COARSE // 2, COARSE), BF)] * 2,
        hbm_outs=[
            shape((CELLS, FINE), BF), shape((WIN, COARSE), BF), shape((WIN, 3 * COARSE), BF),
            shape((4, 4 * WIN, WIN), BF), shape((WIN, COARSE), BF),
        ],
        sems=(8,),
        micros=7,
    )
    other_half = swapped(sent_half)
    (partial,) = call(
        pair_sum, "pair_sum", vmem=(own_half, other_half),
        outs=(shape((COARSE // 2, COARSE), BF),), micros=1,
    )
    sharers = lax.axis_size("lat") * lax.axis_size("lon") // 2
    shares = same_core(partial.reshape(sharers, COARSE // 2 // sharers, COARSE))
    *pieces, coarse_out = call(
        coarse_backward,
        "coarse_backward",
        vmem=(jnp.asarray(PLACE_OF_PARITY),),
        hbm=(cotangent, coarse_proj, c_qkv, c_a, coarse_qkv, merged, fine, merge_weight, c_o),
        outs=piece_shapes(),
        hbm_outs=(shape((6, 12, 2, COARSE), BF),),
        scratch=[pltpu.VMEM((WIN, 3 * COARSE), BF)],
        sems=(18, 1),
        micros=14,
    )
    moved = shifted(pieces, 1)
    (summed,) = call(
        share_sum, "share_sum", vmem=(shares,), outs=(shape(shares.shape, BF),), micros=1,
        after=pieces[3:],
    )
    half = same_core(summed)
    pieces = call(
        fine_backward,
        "fine_backward",
        vmem=(*moved, jnp.asarray(WINDOW_AT), jnp.asarray(PLACE_OF_WINDOW)),
        hbm=(*saved, fine_qkv, fine_proj, fine_up, fine_down),
        outs=piece_shapes(),
        scratch=[pltpu.VMEM((CELLS, 3 * FINE), BF)],
        sems=(23,),
        micros=14,
    )
    half, corner = lax.optimization_barrier((half, pieces[3]))
    moved = shifted([*pieces[:3], corner], -1)
    other = swapped(half)
    (input_grad,) = call(
        unpack, "unpack_grad", vmem=(*moved, jnp.asarray(CELL_AT)),
        hbm_outs=(shape((ROWS, COLS, 2, FINE), F32),), sems=(3,), micros=3,
    )
    proj_grad = half_written(other, half_written(half))
    return coarse_out, input_grad, proj_grad


def solution(mesh):
    field = P("lat", "lon", None, None)
    return jax.shard_map(
        per_device,
        mesh=mesh,
        in_specs=(field, P(), P(), P(), P(), P(), P(), P(), field),
        out_specs=(field, field, P()),
        check_vma=False,
    )
```

```python
import jax
import jax.numpy as jnp
import numpy as np
from jax import lax
from jax.experimental import pallas as pl
from jax.experimental.pallas import tpu as pltpu
from jax.sharding import PartitionSpec as P

BF = jnp.bfloat16
F32 = jnp.float32
ROWS = 12
COLS = 24
CELLS = ROWS * COLS * 2
WIN = 144
HALF_LAT = 3
HALF_LON = 6
FINE = 512
COARSE = 1024
HIDDEN = 2048
QUAD = 256
CHUNK = 512
PIECES = (336, 112, 112, 48)
PACKED = sum(PIECES)
EPS = 1e-05
BOTH = ("lat", "lon")
LIMIT = 26 * 2**20


def cell_orders():
    number = np.arange(CELLS).reshape(ROWS, COLS, 2)
    r, c = ROWS - HALF_LAT, COLS - HALF_LON
    parts = (number[:r, :c], number[:r, c:], number[r:, :c], number[r:, c:])
    pieces = np.full(PACKED, -1)
    start = 0
    for part, room in zip(parts, PIECES):
        pieces[start : start + part.size] = part.reshape(-1)
        start += room
    parity = number.reshape(6, 2, 12, 2, 2).transpose(1, 3, 0, 2, 4).reshape(-1)
    place = np.zeros(CELLS, int)
    place[pieces[pieces >= 0]] = np.nonzero(pieces >= 0)[0]
    place = place.reshape(ROWS, COLS, 2)
    rolled = np.roll(place, (HALF_LAT, HALF_LON), (0, 1))
    window = rolled.reshape(2, 6, 2, 12, 2).transpose(0, 2, 1, 3, 4).reshape(-1)
    return pieces, parity, window


PIECE_CELLS, PARITY_CELLS, WINDOW_PLACES = cell_orders()
PLACE_OF = np.zeros(CELLS, np.int32)
PLACE_OF[PIECE_CELLS[PIECE_CELLS >= 0]] = np.nonzero(PIECE_CELLS >= 0)[0]


def targets(places):
    rows = np.full(PACKED, -1, np.int32)
    rows[places] = np.arange(CELLS, dtype=np.int32)
    return rows.reshape(1, PACKED)


PLACE_OF_PARITY = PLACE_OF[PARITY_CELLS].reshape(1, CELLS)
PLACE_OF_WINDOW = WINDOW_PLACES.astype(np.int32).reshape(1, CELLS)
WINDOW_AT = targets(WINDOW_PLACES)
PARITY_AT = targets(PLACE_OF[PARITY_CELLS])
CELL_AT = targets(PLACE_OF)


def moved_rows(target, values, rows):
    row = lax.broadcasted_iota(jnp.int32, (rows, target.shape[1]), 0)
    return mm(jnp.where(row == target[...], 1.0, 0.0).astype(BF), values)


class Loads:
    def __init__(self, sems, ahead=16 * 2**20):
        self.sems, self.ahead, self.queue, self.started = sems, ahead, [], 0

    def add(self, name, source, target, *where):
        copy = pltpu.make_async_copy(
            source.at[where], target.at[where], self.sems.at[len(self.queue)]
        )
        size = int(np.prod(target.at[where].shape)) * target.dtype.itemsize
        number = len([entry for entry in self.queue if entry[0] == name])
        self.queue.append((name, number, copy, size))

    def start(self, done):
        flying = sum(entry[3] for entry in self.queue[done : self.started])
        while self.started < len(self.queue) and (
            self.started <= done or flying + self.queue[self.started][3] <= self.ahead
        ):
            flying += self.queue[self.started][3]
            self.queue[self.started][2].start()
            self.started += 1

    def wait(self, name, number=0):
        (place,) = [i for i, entry in enumerate(self.queue) if entry[:2] == (name, number)]
        self.start(place)
        self.queue[place][2].wait()
        self.start(place + 1)


class Stores:
    def __init__(self, sems):
        self.sems, self.copies = sems, []

    def start(self, source, target, *where):
        copy = pltpu.make_async_copy(
            source.at[where], target.at[where], self.sems.at[len(self.copies)]
        )
        copy.start()
        self.copies.append(copy)

    def finish(self):
        for copy in self.copies:
            copy.wait()


FULL = slice(None)


def chunk(index, size=CHUNK):
    return pl.ds(index * size, size)


def mm(a, b):
    return jnp.dot(a, b, preferred_element_type=F32)


def mm_nt(a, b):
    return lax.dot_general(a, b, (((1,), (1,)), ((), ())), preferred_element_type=F32)


def mm_tn(a, b):
    return lax.dot_general(a, b, (((0,), (0,)), ((), ())), preferred_element_type=F32)


def normed(values):
    centered = values - jnp.mean(values, axis=-1, keepdims=True)
    scale = lax.rsqrt(jnp.mean(centered * centered, axis=-1, keepdims=True) + EPS)
    return centered * scale, scale


def normed_pull(unit, scale, grad):
    low = jnp.mean(grad, axis=-1, keepdims=True)
    along = jnp.mean(grad * unit, axis=-1, keepdims=True)
    return scale * (grad - low - unit * along)


def heads_apart(values):
    head = lax.broadcasted_iota(jnp.int32, values.shape, 1) // 64
    zero = jnp.zeros_like(values)
    return jnp.concatenate([jnp.where(head == h, values, zero) for h in range(4)], axis=0)


def heads_joined(stacked):
    rows = stacked.shape[0] // 4
    head = lax.broadcasted_iota(jnp.int32, (rows, QUAD), 1) // 64
    out = stacked[:rows]
    for h in range(1, 4):
        out = jnp.where(head == h, stacked[h * rows : (h + 1) * rows], out)
    return out


def attend(q, k, v, bias):
    apart = heads_apart(q * 0.125)
    scores = mm_nt(apart, k)
    if bias is not None:
        scores = scores + bias
    weights = jnp.exp(scores - jnp.max(scores, axis=-1, keepdims=True))
    a = (weights * (1.0 / jnp.sum(weights, axis=-1, keepdims=True))).astype(BF)
    return a, heads_joined(mm(a, v)).astype(BF)


def attend_pull(q, k, v, a, grad):
    apart = heads_apart(grad)
    af = a.astype(F32)
    weighted = mm_nt(apart, v) * af
    ds = (weighted - af * jnp.sum(weighted, axis=-1, keepdims=True)).astype(BF)
    dq = heads_joined(mm(ds, k)) * 0.125
    dk = mm_tn(ds, heads_apart(q * 0.125))
    dv = mm_tn(a, apart)
    return dq.astype(BF), dk.astype(BF), dv.astype(BF)


def gelu_pair(h):
    cdf = 0.5 * (1.0 + lax.erf(h * 0.7071067811865476))
    return h * cdf, cdf + h * (0.3989422804014327 * jnp.exp(-0.5 * h * h))


def split_pieces(packed, refs):
    start = 0
    for ref, room in zip(refs, PIECES):
        ref[...] = packed[start : start + room].astype(ref.dtype)
        start += room


def joined_pieces(refs):
    return jnp.concatenate([ref[...] for ref in refs], axis=0)


def fine_forward(
    keep, beside, above, corner, window_at, place_of_window, qkv_w, proj_w, up_w, down_w,
    out0, out1, out2, out3, x_hbm, qkv_hbm, a_hbm, att_hbm, slope_hbm,
    x_out, qkv_out, a_out, att_out, slope_out, mixed, sems
):
    stores = Stores(sems)
    x = moved_rows(window_at, joined_pieces((keep, beside, above, corner)), CELLS)
    x_out[...] = x.astype(BF)
    stores.start(x_out, x_hbm)
    unit, _ = normed(x)
    unit = unit.astype(BF)
    for i in range(3):
        qkv_out[:, chunk(i)] = mm(unit, qkv_w[:, chunk(i)]).astype(BF)
    stores.start(qkv_out, qkv_hbm)
    half_q = (lax.broadcasted_iota(jnp.int32, (4 * WIN, WIN), 0) % WIN) >= WIN // 2
    half_k = lax.broadcasted_iota(jnp.int32, (4 * WIN, WIN), 1) >= WIN // 2
    apart = jnp.where(lax.axis_index("lat") == 0, -1e30, 0.0)
    bias = jnp.where(half_q != half_k, apart, 0.0)
    for w in range(4):
        for g in range(2):
            rows, cols = slice(w * WIN, (w + 1) * WIN), g * QUAD
            a, o = attend(
                qkv_out[rows, cols : cols + QUAD],
                qkv_out[rows, FINE + cols : FINE + cols + QUAD],
                qkv_out[rows, 2 * FINE + cols : 2 * FINE + cols + QUAD],
                bias if w < 2 else None,
            )
            a_out[2 * w + g] = a
            mixed[rows, cols : cols + QUAD] = o
        stores.start(a_out, a_hbm, pl.ds(2 * w, 2))
    attended = x + mm(mixed[...], proj_w[...])
    att_out[...] = attended
    stores.start(att_out, att_hbm)
    unit, _ = normed(attended)
    unit = unit.astype(BF)
    total = attended
    for c in range(HIDDEN // CHUNK):
        value, slope = gelu_pair(mm(unit, up_w[:, chunk(c)]))
        slope_out[:, chunk(c)] = slope.astype(BF)
        stores.start(slope_out, slope_hbm, FULL, chunk(c))
        total = total + mm(value.astype(BF), down_w[chunk(c)])
    split_pieces(
        moved_rows(place_of_window, total.astype(BF), PACKED), (out0, out1, out2, out3)
    )
    stores.finish()


def merge_unit(parts):
    mean = sum(jnp.sum(part, axis=-1, keepdims=True) for part in parts) / (4 * FINE)
    parts = [part - mean for part in parts]
    spread = sum(jnp.sum(part * part, axis=-1, keepdims=True) for part in parts) / (4 * FINE)
    scale = lax.rsqrt(spread + EPS)
    return [part * scale for part in parts], scale


def coarse_forward(
    keep, beside, above, corner, parity_at, merge_w, qkv_w, cot_in,
    own_half, sent_half, fine_hbm, merged_hbm, qkv_hbm, a_hbm, o_hbm,
    fine_out, merged_out, qkv_out, a_out, mixed, sems
):
    stores = Stores(sems)
    fine = moved_rows(parity_at, joined_pieces((keep, beside, above, corner)), CELLS)
    fine_out[...] = fine.astype(BF)
    stores.start(fine_out, fine_hbm)
    units, _ = merge_unit([fine[p * WIN : (p + 1) * WIN] for p in range(4)])
    merged = jnp.zeros((WIN, COARSE), F32)
    for p in range(4):
        merged = merged + mm(units[p].astype(BF), merge_w[chunk(p)])
    merged = merged.astype(BF)
    merged_out[...] = merged
    stores.start(merged_out, merged_hbm)
    unit, _ = normed(merged.astype(F32))
    unit = unit.astype(BF)
    for i in range(3):
        qkv_out[:, chunk(i, COARSE)] = mm(unit, qkv_w[:, chunk(i, COARSE)]).astype(BF)
    stores.start(qkv_out, qkv_hbm)
    cot = cot_in[...].reshape(WIN, COARSE).astype(BF)
    for g in range(4):
        cols = g * QUAD
        a, o = attend(
            qkv_out[:, cols : cols + QUAD],
            qkv_out[:, COARSE + cols : COARSE + cols + QUAD],
            qkv_out[:, 2 * COARSE + cols : 2 * COARSE + cols + QUAD],
            None,
        )
        a_out[g] = a
        mixed[:, cols : cols + QUAD] = o
        stores.start(a_out, a_hbm, pl.ds(g, 1))
    stores.start(mixed, o_hbm)
    first = lax.axis_index("lat") % 2 == 0
    low = mm_tn(mixed[:, : COARSE // 2], cot) * 18432.0 ** (-0.5)
    high = mm_tn(mixed[:, COARSE // 2 :], cot) * 18432.0 ** (-0.5)
    own_half[...] = jnp.where(first, low, high).astype(BF)
    sent_half[...] = jnp.where(first, high, low).astype(BF)
    stores.finish()


def coarse_backward(
    place_of_parity, cot_hbm, proj_hbm, qkv_res, a_hbm, qkv_hbm, merged_hbm, fine_hbm, merge_hbm, o_hbm,
    out0, out1, out2, out3, out_hbm,
    cot_in, proj_w, qkv, a, qkv_w, merged, fine, merge_w, o, coarse_out, dqkv, in_sems, out_sems
):
    loads, stores = Loads(in_sems), Stores(out_sems)
    loads.add("cot", cot_hbm, cot_in)
    for i in range(2):
        loads.add("proj", proj_hbm, proj_w, chunk(i))
    loads.add("qkv", qkv_res, qkv)
    for g in range(4):
        loads.add("a", a_hbm, a, pl.ds(g, 1))
    loads.add("merged", merged_hbm, merged)
    loads.add("o", o_hbm, o)
    for i in range(3):
        loads.add("qkv_w", qkv_hbm, qkv_w, FULL, chunk(i, COARSE))
    loads.add("fine", fine_hbm, fine)
    for p in range(4):
        loads.add("merge", merge_hbm, merge_w, chunk(p))
    loads.start(0)
    loads.wait("cot")
    cot = cot_in[...].reshape(WIN, COARSE)
    cot_b = cot.astype(BF)
    grads = []
    for i in range(2):
        loads.wait("proj", i)
        grads.append(mm_nt(cot_b, proj_w[chunk(i)]).astype(BF))
    grad = jnp.concatenate(grads, axis=1)
    loads.wait("qkv")
    for g in range(4):
        loads.wait("a", g)
        cols = g * QUAD
        pulled = attend_pull(
            qkv[:, cols : cols + QUAD],
            qkv[:, COARSE + cols : COARSE + cols + QUAD],
            qkv[:, 2 * COARSE + cols : 2 * COARSE + cols + QUAD],
            a[g],
            grad[:, cols : cols + QUAD],
        )
        for i in range(3):
            dqkv[:, i * COARSE + cols : i * COARSE + cols + QUAD] = pulled[i]
    loads.wait("merged")
    loads.wait("o")
    merged_f = merged[...].astype(F32)
    full = (merged_f + mm(o[...], proj_w[...])).astype(BF)
    coarse_out[...] = full.astype(F32).reshape(coarse_out.shape).astype(BF)
    stores.start(coarse_out, out_hbm)
    dn = jnp.zeros((WIN, COARSE), F32)
    for i in range(3):
        loads.wait("qkv_w", i)
        dn = dn + mm_nt(dqkv[:, chunk(i, COARSE)], qkv_w[:, chunk(i, COARSE)])
    dn = dn.astype(BF).astype(F32)
    unit, scale = normed(merged_f)
    merged_grad = (cot + normed_pull(unit, scale, dn)).astype(BF)
    loads.wait("fine")
    units, scale = merge_unit([fine[p * WIN : (p + 1) * WIN].astype(F32) for p in range(4)])
    grads = []
    for p in range(4):
        loads.wait("merge", p)
        grads.append(mm_nt(merged_grad, merge_w[chunk(p)]).astype(BF).astype(F32))
    low = sum(jnp.sum(g, axis=-1, keepdims=True) for g in grads) / (4 * FINE)
    along = sum(jnp.sum(g * u, axis=-1, keepdims=True) for g, u in zip(grads, units)) / (4 * FINE)
    fine_grad = jnp.concatenate(
        [(scale * (g - low - u * along)).astype(BF) for g, u in zip(grads, units)], axis=0
    )
    split_pieces(moved_rows(place_of_parity, fine_grad, PACKED), (out0, out1, out2, out3))
    stores.finish()


def fine_backward(
    keep, beside, above, corner, window_at, place_of_window,
    x_hbm, qkv_res, a_hbm, att_hbm, slope_hbm, qkv_hbm, proj_hbm, up_hbm, down_hbm,
    out0, out1, out2, out3,
    x, qkv, a, att, slope, qkv_w, proj_w, up_w, down_w, dqkv, incoming, rounded, dn, grad,
    hidden_sems, window_sems, sems
):
    hidden_steps = HIDDEN // CHUNK

    def hidden_copies(c):
        cols = pl.ds(pl.multiple_of(c * CHUNK, CHUNK), CHUNK)
        return (
            pltpu.make_async_copy(down_hbm.at[cols], down_w.at[cols], hidden_sems.at[c, 0]),
            pltpu.make_async_copy(slope_hbm.at[:, cols], slope.at[:, cols], hidden_sems.at[c, 1]),
            pltpu.make_async_copy(up_hbm.at[:, cols], up_w.at[:, cols], hidden_sems.at[c, 2]),
        )

    def window_copies(w):
        pair = pl.ds(2 * w, 2)
        rows = pl.ds(pl.multiple_of(w * WIN, WIN), WIN)
        return (
            pltpu.make_async_copy(a_hbm.at[pair], a.at[pair], window_sems.at[w, 0]),
            pltpu.make_async_copy(qkv_res.at[rows], qkv.at[rows], window_sems.at[w, 1]),
        )

    att_copy = pltpu.make_async_copy(att_hbm, att, sems.at[0])
    proj_copy = pltpu.make_async_copy(proj_hbm, proj_w, sems.at[1])
    qkv_copy = pltpu.make_async_copy(qkv_hbm, qkv_w, sems.at[2])
    x_copy = pltpu.make_async_copy(x_hbm, x, sems.at[3])
    for c in range(2):
        for copy in hidden_copies(c):
            copy.start()
    arrived = moved_rows(window_at, joined_pieces((keep, beside, above, corner)), CELLS)
    incoming[...] = arrived
    rounded[...] = arrived.astype(BF)
    dn[...] = jnp.zeros_like(dn)

    @pl.loop(0, hidden_steps)
    def _(c):
        for copy in hidden_copies(c):
            copy.wait()

        @pl.when(c + 2 < hidden_steps)
        def _():
            for copy in hidden_copies(c + 2):
                copy.start()

        @pl.when(c + 2 == hidden_steps)
        def _():
            att_copy.start()
            proj_copy.start()

        @pl.when(c + 1 == hidden_steps)
        def _():
            for copy in (*window_copies(0), *window_copies(1)):
                copy.start()

        cols = pl.ds(pl.multiple_of(c * CHUNK, CHUNK), CHUNK)
        dh = mm_nt(rounded[...], down_w[cols]) * slope[:, cols].astype(F32)
        dn[...] += mm_nt(dh.astype(BF), up_w[:, cols])

    att_copy.wait()
    proj_copy.wait()
    unit, scale = normed(att[...])
    att_grad = incoming[...] + normed_pull(unit, scale, dn[...])
    incoming[...] = att_grad
    grad[...] = mm_nt(att_grad.astype(BF), proj_w[...]).astype(BF)

    @pl.loop(0, 4)
    def _(w):
        for copy in window_copies(w):
            copy.wait()

        @pl.when(w < 2)
        def _():
            for copy in window_copies(w + 2):
                copy.start()

        @pl.when(w == 2)
        def _():
            qkv_copy.start()
            x_copy.start()

        rows = pl.ds(pl.multiple_of(w * WIN, WIN), WIN)
        for g in range(2):
            cols = g * QUAD
            pulled = attend_pull(
                qkv[rows, cols : cols + QUAD],
                qkv[rows, FINE + cols : FINE + cols + QUAD],
                qkv[rows, 2 * FINE + cols : 2 * FINE + cols + QUAD],
                a[2 * w + g],
                grad[rows, cols : cols + QUAD],
            )
            for i in range(3):
                dqkv[rows, i * FINE + cols : i * FINE + cols + QUAD] = pulled[i]

    qkv_copy.wait()
    x_copy.wait()
    back = mm_nt(dqkv[...], qkv_w[...])
    unit, scale = normed(x[...].astype(F32))
    total = incoming[...] + normed_pull(unit, scale, back)
    split_pieces(
        moved_rows(place_of_window, total.astype(BF), PACKED), (out0, out1, out2, out3)
    )


def pack(cells, out0, out1, out2, out3):
    cell = lax.broadcasted_iota(jnp.int32, (1, CELLS), 1)
    line, kept = 2 * COLS, 2 * (COLS - HALF_LON)
    row = sum((cell >= line * r).astype(jnp.int32) for r in range(1, ROWS))
    across = cell - line * row
    rest, side = row - (ROWS - HALF_LAT), across - kept
    starts = [sum(PIECES[:i]) for i in range(4)]
    inner = jnp.where(side < 0, row * kept + across, starts[1] + row * (line - kept) + side)
    outer = jnp.where(
        side < 0, starts[2] + rest * kept + across, starts[3] + rest * (line - kept) + side
    )
    place = jnp.where(rest < 0, inner, outer)
    flat = cells[...].reshape(CELLS, FINE)
    split_pieces(moved_rows(place, flat, PACKED), (out0, out1, out2, out3))


def fetch(*refs):
    count = (len(refs) - 1) // 2
    copies = [
        pltpu.make_async_copy(refs[i], refs[count + i], refs[-1].at[i]) for i in range(count)
    ]
    for copy in copies:
        copy.start()
    for copy in copies:
        copy.wait()


def unpack(keep, beside, above, corner, cell_at, out_hbm, out, sems):
    stores = Stores(sems)
    pieces = joined_pieces((keep, beside, above, corner))
    cells = moved_rows(cell_at, pieces, CELLS)
    part = ROWS // 3
    for i in range(3):
        rows = cells[i * CELLS // 3 : (i + 1) * CELLS // 3]
        out[pl.ds(i * part, part)] = rows.reshape(part, COLS, 2, FINE)
        stores.start(out, out_hbm, pl.ds(i * part, part))
    stores.finish()


def pair_sum(own, other, out):
    out[...] = (own[...].astype(F32) + other[...].astype(F32)).astype(BF)


def share_sum(parts, after, out):
    total = parts[0].astype(F32)
    for i in range(1, parts.shape[0]):
        total = total + parts[i].astype(F32)
    total = total.astype(BF)
    for i in range(parts.shape[0]):
        out[i] = total


def write_half(half, rows, out_hbm, wide, sems):
    stores = Stores(sems)
    part = COARSE // 8
    for i in range(4):
        wide[pl.ds(i * part, part)] = half[pl.ds(i * part, part)].astype(F32)
        copy = pltpu.make_async_copy(
            wide.at[pl.ds(i * part, part)],
            out_hbm.at[pl.ds(pl.multiple_of(rows + i * part, part), part)],
            sems.at[i],
        )
        copy.start()
        stores.copies.append(copy)
    stores.finish()


def first_half(half, out_hbm, wide, sems):
    write_half(half, (lax.axis_index("lat") % 2) * (COARSE // 2), out_hbm, wide, sems)


def second_half(half, begun, out_hbm, wide, sems):
    write_half(half, (1 - lax.axis_index("lat") % 2) * (COARSE // 2), out_hbm, wide, sems)


def compiler_params():
    return pltpu.CompilerParams(vmem_limit_bytes=LIMIT)


def cost(micros, operands, outs):
    moved = sum(int(np.prod(o.shape)) * o.dtype.itemsize for o in jax.tree.leaves((operands, outs)))
    return pl.CostEstimate(
        flops=micros * 1153 * 10**6, bytes_accessed=moved, transcendentals=0
    )


def call(body, name, smem=(), vmem=(), hbm=(), outs=(), hbm_outs=(), scratch=(), sems=(), micros=1, after=()):
    hbm = [pltpu.with_memory_space_constraint(o, pltpu.HBM) for o in hbm]
    operands = [*smem, *vmem, *hbm]
    staged = [pltpu.VMEM(o.shape, o.dtype) for o in [*hbm, *hbm_outs]]
    waits = list(after)
    spaces = [pltpu.SMEM] * len(smem) + [pltpu.VMEM] * len(vmem) + [pltpu.HBM] * len(hbm)
    spaces += [pltpu.VMEM] * len(waits)
    results = [pltpu.VMEM] * len(outs) + [pltpu.HBM] * len(hbm_outs)
    return pl.pallas_call(
        body,
        name=name,
        out_shape=[
            *[pltpu.VMEM(o.shape, o.dtype) for o in outs], *[pltpu.HBM(o.shape, o.dtype) for o in hbm_outs]
        ],
        in_specs=[pl.BlockSpec(memory_space=space) for space in spaces],
        out_specs=[pl.BlockSpec(memory_space=space) for space in results],
        scratch_shapes=[*staged, *scratch] + ([pltpu.SemaphoreType.DMA(n if isinstance(n, tuple) else (n,)) for n in sems]),
        compiler_params=compiler_params(),
        cost_estimate=cost(micros, operands, [*outs, *hbm_outs]),
    )(*operands, *waits)


def fetched(name, arrays, after=None, micros=2):
    hbm = [pltpu.with_memory_space_constraint(array, pltpu.HBM) for array in arrays]
    spec = [pl.BlockSpec(memory_space=pltpu.HBM)] * len(hbm)
    waits = [] if after is None else [after]

    def body(*refs):
        fetch(*refs[: len(hbm)], *refs[len(hbm) + len(waits) :])

    return pl.pallas_call(
        body,
        name=name,
        out_shape=[pltpu.VMEM(array.shape, array.dtype) for array in arrays],
        in_specs=spec + [pl.BlockSpec(memory_space=pltpu.VMEM)] * len(waits),
        out_specs=[pl.BlockSpec(memory_space=pltpu.VMEM)] * len(hbm),
        scratch_shapes=[pltpu.SemaphoreType.DMA((len(hbm),))],
        compiler_params=compiler_params(),
        cost_estimate=cost(micros, arrays, arrays),
    )(*hbm, *waits)


def half_written(half, begun=None):
    half = half.reshape(COARSE // 2, COARSE)
    hbm = pl.BlockSpec(memory_space=pltpu.HBM)
    last = begun is not None
    return pl.pallas_call(
        second_half if last else first_half,
        name="second_half" if last else "first_half",
        out_shape=pltpu.HBM((COARSE, COARSE), F32),
        in_specs=[pl.BlockSpec(memory_space=pltpu.VMEM)] + [hbm] * last,
        out_specs=hbm,
        input_output_aliases={1: 0} if last else {},
        scratch_shapes=[pltpu.VMEM((COARSE // 2, COARSE), F32), pltpu.SemaphoreType.DMA((4,))],
        compiler_params=compiler_params(),
        cost_estimate=cost(2, half, half),
    )(half, *([begun] if last else []))


def piece_shapes():
    return [jax.ShapeDtypeStruct((room, FINE), BF) for room in PIECES]


def shifted(pieces, sign):
    lat_count, lon_count = lax.axis_size("lat"), lax.axis_size("lon")
    moved = [pieces[0]]
    for piece, (up, side) in zip(pieces[1:], ((0, 1), (1, 0), (1, 1))):
        pairs = []
        for i in range(lat_count):
            for j in range(lon_count):
                to = (i + sign * up) % lat_count, (j + sign * side) % lon_count
                pairs.append((i * lon_count + j, to[0] * lon_count + to[1]))
        moved.append(lax.ppermute(piece, BOTH, pairs))
    return moved


def swapped(values):
    return lax.ppermute(values, "lat", [(i, i ^ 1) for i in range(lax.axis_size("lat"))])


def same_core(values):
    lat_count, lon_count = lax.axis_size("lat"), lax.axis_size("lon")
    groups = [
        [i * lon_count + j for i in range(c, lat_count, 2) for j in range(lon_count)]
        for c in range(2)
    ]
    return lax.all_to_all(values, BOTH, 0, 0, tiled=True, axis_index_groups=groups)


def per_device(
    tokens, fine_qkv, fine_proj, fine_up, fine_down, merge_weight, coarse_qkv, coarse_proj, cotangent
):
    shape = jax.ShapeDtypeStruct
    pieces = call(
        pack, "pack_tokens", vmem=(tokens,),
        outs=piece_shapes(), micros=2,
    )
    *fine_weights, merge_w = fetched(
        "fetch_fine", (fine_qkv, fine_proj, fine_up, fine_down, merge_weight), after=pieces[3], micros=4
    )
    moved = shifted(pieces, 1)
    results = call(
        fine_forward,
        "fine_forward",
        vmem=(*moved, jnp.asarray(WINDOW_AT), jnp.asarray(PLACE_OF_WINDOW), *fine_weights),
        outs=piece_shapes(),
        hbm_outs=[
            shape((CELLS, FINE), BF), shape((CELLS, 3 * FINE), BF), shape((8, 4 * WIN, WIN), BF),
            shape((CELLS, FINE), F32), shape((CELLS, HIDDEN), BF),
        ],
        scratch=[pltpu.VMEM((CELLS, FINE), BF)],
        sems=(11,),
        micros=9,
    )
    pieces, saved = results[:4], results[4:]
    coarse_weights = fetched(
        "fetch_coarse", (coarse_qkv, cotangent), after=pieces[3], micros=3
    )
    moved = shifted(pieces, -1)
    own_half, sent_half, fine, merged, c_qkv, c_a, c_o = call(
        coarse_forward,
        "coarse_forward",
        vmem=(*moved, jnp.asarray(PARITY_AT), merge_w, *coarse_weights),
        outs=[shape((COARSE // 2, COARSE), BF)] * 2,
        hbm_outs=[
            shape((CELLS, FINE), BF), shape((WIN, COARSE), BF), shape((WIN, 3 * COARSE), BF),
            shape((4, 4 * WIN, WIN), BF), shape((WIN, COARSE), BF),
        ],
        sems=(8,),
        micros=7,
    )
    other_half = swapped(sent_half)
    (partial,) = call(
        pair_sum, "pair_sum", vmem=(own_half, other_half),
        outs=(shape((COARSE // 2, COARSE), BF),), micros=1,
    )
    sharers = lax.axis_size("lat") * lax.axis_size("lon") // 2
    shares = same_core(partial.reshape(sharers, COARSE // 2 // sharers, COARSE))
    *pieces, coarse_out = call(
        coarse_backward,
        "coarse_backward",
        vmem=(jnp.asarray(PLACE_OF_PARITY),),
        hbm=(cotangent, coarse_proj, c_qkv, c_a, coarse_qkv, merged, fine, merge_weight, c_o),
        outs=piece_shapes(),
        hbm_outs=(shape((6, 12, 2, COARSE), BF),),
        scratch=[pltpu.VMEM((WIN, 3 * COARSE), BF)],
        sems=(18, 1),
        micros=14,
    )
    moved = shifted(pieces, 1)
    (summed,) = call(
        share_sum, "share_sum", vmem=(shares,), outs=(shape(shares.shape, BF),), micros=1,
        after=pieces[3:],
    )
    half = same_core(summed)
    pieces = call(
        fine_backward,
        "fine_backward",
        vmem=(*moved, jnp.asarray(WINDOW_AT), jnp.asarray(PLACE_OF_WINDOW)),
        hbm=(*saved, fine_qkv, fine_proj, fine_up, fine_down),
        outs=piece_shapes(),
        scratch=[
            pltpu.VMEM((CELLS, 3 * FINE), BF), pltpu.VMEM((CELLS, FINE), F32), pltpu.VMEM((CELLS, FINE), BF),
            pltpu.VMEM((CELLS, FINE), F32), pltpu.VMEM((CELLS, FINE), BF),
        ],
        sems=((HIDDEN // CHUNK, 3), (4, 2), (4,)),
        micros=14,
    )
    begun = half_written(half)
    kept, *arrived = shifted(pieces, -1)
    half, begun, *arrived = lax.optimization_barrier((half, begun, *arrived))
    moved = [kept, *arrived]
    other = swapped(half)
    (input_grad,) = call(
        unpack, "unpack_grad", vmem=(*moved, jnp.asarray(CELL_AT)),
        hbm_outs=(shape((ROWS, COLS, 2, FINE), F32),), sems=(3,), micros=3,
    )
    proj_grad = half_written(other, begun)
    return coarse_out, input_grad, proj_grad


def solution(mesh):
    field = P("lat", "lon", None, None)
    return jax.shard_map(
        per_device,
        mesh=mesh,
        in_specs=(field, P(), P(), P(), P(), P(), P(), P(), field),
        out_specs=(field, field, P()),
        check_vma=False,
    )
```

```python
import jax
import jax.numpy as jnp
import numpy as np
from jax import lax
from jax.experimental import pallas as pl
from jax.experimental.pallas import tpu as pltpu
from jax.sharding import PartitionSpec as P

BF = jnp.bfloat16
F32 = jnp.float32
ROWS = 12
COLS = 24
CELLS = ROWS * COLS * 2
WIN = 144
HALF_LAT = 3
HALF_LON = 6
FINE = 512
COARSE = 1024
HIDDEN = 2048
QUAD = 256
CHUNK = 512
WIDE = 1024
PIECES = (336, 112, 112, 48)
PACKED = sum(PIECES)
EPS = 1e-05
BOTH = ("lat", "lon")
LIMIT = 26 * 2**20


def cell_orders():
    number = np.arange(CELLS).reshape(ROWS, COLS, 2)
    r, c = ROWS - HALF_LAT, COLS - HALF_LON
    parts = (number[:r, :c], number[:r, c:], number[r:, :c], number[r:, c:])
    pieces = np.full(PACKED, -1)
    start = 0
    for part, room in zip(parts, PIECES):
        pieces[start : start + part.size] = part.reshape(-1)
        start += room
    parity = number.reshape(6, 2, 12, 2, 2).transpose(1, 3, 0, 2, 4).reshape(-1)
    place = np.zeros(CELLS, int)
    place[pieces[pieces >= 0]] = np.nonzero(pieces >= 0)[0]
    place = place.reshape(ROWS, COLS, 2)
    rolled = np.roll(place, (HALF_LAT, HALF_LON), (0, 1))
    window = rolled.reshape(2, 6, 2, 12, 2).transpose(0, 2, 1, 3, 4).reshape(-1)
    return pieces, parity, window


PIECE_CELLS, PARITY_CELLS, WINDOW_PLACES = cell_orders()
PLACE_OF = np.zeros(CELLS, np.int32)
PLACE_OF[PIECE_CELLS[PIECE_CELLS >= 0]] = np.nonzero(PIECE_CELLS >= 0)[0]


def targets(places):
    rows = np.full(PACKED, -1, np.int32)
    rows[places] = np.arange(CELLS, dtype=np.int32)
    return rows.reshape(1, PACKED)


PLACE_OF_PARITY = PLACE_OF[PARITY_CELLS].reshape(1, CELLS)
PLACE_OF_WINDOW = WINDOW_PLACES.astype(np.int32).reshape(1, CELLS)
WINDOW_AT = targets(WINDOW_PLACES)
PARITY_AT = targets(PLACE_OF[PARITY_CELLS])
CELL_AT = targets(PLACE_OF)


def moved_rows(target, values, rows):
    row = lax.broadcasted_iota(jnp.int32, (rows, target.shape[1]), 0)
    return mm(jnp.where(row == target[...], 1.0, 0.0).astype(BF), values)


class Loads:
    def __init__(self, sems, ahead=16 * 2**20):
        self.sems, self.ahead, self.queue, self.started = sems, ahead, [], 0

    def add(self, name, source, target, *where):
        copy = pltpu.make_async_copy(
            source.at[where], target.at[where], self.sems.at[len(self.queue)]
        )
        size = int(np.prod(target.at[where].shape)) * target.dtype.itemsize
        number = len([entry for entry in self.queue if entry[0] == name])
        self.queue.append((name, number, copy, size))

    def start(self, done):
        flying = sum(entry[3] for entry in self.queue[done : self.started])
        while self.started < len(self.queue) and (
            self.started <= done or flying + self.queue[self.started][3] <= self.ahead
        ):
            flying += self.queue[self.started][3]
            self.queue[self.started][2].start()
            self.started += 1

    def wait(self, name, number=0):
        (place,) = [i for i, entry in enumerate(self.queue) if entry[:2] == (name, number)]
        self.start(place)
        self.queue[place][2].wait()
        self.start(place + 1)


class Stores:
    def __init__(self, sems):
        self.sems, self.copies = sems, []

    def start(self, source, target, *where):
        copy = pltpu.make_async_copy(
            source.at[where], target.at[where], self.sems.at[len(self.copies)]
        )
        copy.start()
        self.copies.append(copy)

    def finish(self):
        for copy in self.copies:
            copy.wait()


FULL = slice(None)


def chunk(index, size=CHUNK):
    return pl.ds(index * size, size)


def mm(a, b):
    return jnp.dot(a, b, preferred_element_type=F32)


def mm_nt(a, b):
    return lax.dot_general(a, b, (((1,), (1,)), ((), ())), preferred_element_type=F32)


def mm_tn(a, b):
    return lax.dot_general(a, b, (((0,), (0,)), ((), ())), preferred_element_type=F32)


def normed(values):
    centered = values - jnp.mean(values, axis=-1, keepdims=True)
    scale = lax.rsqrt(jnp.mean(centered * centered, axis=-1, keepdims=True) + EPS)
    return centered * scale, scale


def normed_pull(unit, scale, grad):
    low = jnp.mean(grad, axis=-1, keepdims=True)
    along = jnp.mean(grad * unit, axis=-1, keepdims=True)
    return scale * (grad - low - unit * along)


def heads_apart(values):
    head = lax.broadcasted_iota(jnp.int32, values.shape, 1) // 64
    zero = jnp.zeros_like(values)
    return jnp.concatenate([jnp.where(head == h, values, zero) for h in range(4)], axis=0)


def heads_joined(stacked):
    rows = stacked.shape[0] // 4
    head = lax.broadcasted_iota(jnp.int32, (rows, QUAD), 1) // 64
    out = stacked[:rows]
    for h in range(1, 4):
        out = jnp.where(head == h, stacked[h * rows : (h + 1) * rows], out)
    return out


def attend(q, k, v, bias):
    apart = heads_apart(q * 0.125)
    scores = mm_nt(apart, k)
    if bias is not None:
        scores = scores + bias
    weights = jnp.exp(scores - jnp.max(scores, axis=-1, keepdims=True))
    a = (weights * (1.0 / jnp.sum(weights, axis=-1, keepdims=True))).astype(BF)
    return a, heads_joined(mm(a, v)).astype(BF)


def attend_pull(q, k, v, a, grad):
    apart = heads_apart(grad)
    af = a.astype(F32)
    weighted = mm_nt(apart, v) * af
    ds = (weighted - af * jnp.sum(weighted, axis=-1, keepdims=True)).astype(BF)
    dq = heads_joined(mm(ds, k)) * 0.125
    dk = mm_tn(ds, heads_apart(q * 0.125))
    dv = mm_tn(a, apart)
    return dq.astype(BF), dk.astype(BF), dv.astype(BF)


def gelu_pair(h):
    cdf = 0.5 * (1.0 + lax.erf(h * 0.7071067811865476))
    return h * cdf, cdf + h * (0.3989422804014327 * jnp.exp(-0.5 * h * h))


def split_pieces(packed, refs):
    start = 0
    for ref, room in zip(refs, PIECES):
        ref[...] = packed[start : start + room].astype(ref.dtype)
        start += room


def joined_pieces(refs):
    return jnp.concatenate([ref[...] for ref in refs], axis=0)


def fine_forward(
    keep, beside, above, corner, window_at, place_of_window, qkv_w, proj_w, up_w, down_w,
    out0, out1, out2, out3, x_hbm, qkv_hbm, a_hbm, att_hbm, slope_hbm,
    x_out, qkv_out, a_out, att_out, slope_out, mixed, sems
):
    stores = Stores(sems)
    x = moved_rows(window_at, joined_pieces((keep, beside, above, corner)), CELLS)
    x_out[...] = x.astype(BF)
    stores.start(x_out, x_hbm)
    unit, _ = normed(x)
    unit = unit.astype(BF)
    for i in range(3):
        qkv_out[:, chunk(i)] = mm(unit, qkv_w[:, chunk(i)]).astype(BF)
    stores.start(qkv_out, qkv_hbm)
    half_q = (lax.broadcasted_iota(jnp.int32, (4 * WIN, WIN), 0) % WIN) >= WIN // 2
    half_k = lax.broadcasted_iota(jnp.int32, (4 * WIN, WIN), 1) >= WIN // 2
    apart = jnp.where(lax.axis_index("lat") == 0, -1e30, 0.0)
    bias = jnp.where(half_q != half_k, apart, 0.0)
    for w in range(4):
        for g in range(2):
            rows, cols = slice(w * WIN, (w + 1) * WIN), g * QUAD
            a, o = attend(
                qkv_out[rows, cols : cols + QUAD],
                qkv_out[rows, FINE + cols : FINE + cols + QUAD],
                qkv_out[rows, 2 * FINE + cols : 2 * FINE + cols + QUAD],
                bias if w < 2 else None,
            )
            a_out[2 * w + g] = a
            mixed[rows, cols : cols + QUAD] = o
        stores.start(a_out, a_hbm, pl.ds(2 * w, 2))
    attended = x + mm(mixed[...], proj_w[...])
    att_out[...] = attended
    stores.start(att_out, att_hbm)
    unit, _ = normed(attended)
    unit = unit.astype(BF)
    total = attended
    for c in range(HIDDEN // WIDE):
        value, slope = gelu_pair(mm(unit, up_w[:, chunk(c, WIDE)]))
        slope_out[:, chunk(c, WIDE)] = slope.astype(BF)
        stores.start(slope_out, slope_hbm, FULL, chunk(c, WIDE))
        total = total + mm(value.astype(BF), down_w[chunk(c, WIDE)])
    split_pieces(
        moved_rows(place_of_window, total.astype(BF), PACKED), (out0, out1, out2, out3)
    )
    stores.finish()


def merge_unit(parts):
    mean = sum(jnp.sum(part, axis=-1, keepdims=True) for part in parts) / (4 * FINE)
    parts = [part - mean for part in parts]
    spread = sum(jnp.sum(part * part, axis=-1, keepdims=True) for part in parts) / (4 * FINE)
    scale = lax.rsqrt(spread + EPS)
    return [part * scale for part in parts], scale


def coarse_forward(
    keep, beside, above, corner, parity_at, merge_w, qkv_w, cot_in,
    own_half, sent_half, fine_hbm, merged_hbm, qkv_hbm, a_hbm, o_hbm,
    fine_out, merged_out, qkv_out, a_out, mixed, sems
):
    stores = Stores(sems)
    fine = moved_rows(parity_at, joined_pieces((keep, beside, above, corner)), CELLS)
    fine_out[...] = fine.astype(BF)
    stores.start(fine_out, fine_hbm)
    units, _ = merge_unit([fine[p * WIN : (p + 1) * WIN] for p in range(4)])
    merged = jnp.zeros((WIN, COARSE), F32)
    for p in range(4):
        merged = merged + mm(units[p].astype(BF), merge_w[chunk(p)])
    merged = merged.astype(BF)
    merged_out[...] = merged
    stores.start(merged_out, merged_hbm)
    unit, _ = normed(merged.astype(F32))
    unit = unit.astype(BF)
    for i in range(3):
        qkv_out[:, chunk(i, COARSE)] = mm(unit, qkv_w[:, chunk(i, COARSE)]).astype(BF)
    stores.start(qkv_out, qkv_hbm)
    cot = cot_in[...].reshape(WIN, COARSE).astype(BF)
    for g in range(4):
        cols = g * QUAD
        a, o = attend(
            qkv_out[:, cols : cols + QUAD],
            qkv_out[:, COARSE + cols : COARSE + cols + QUAD],
            qkv_out[:, 2 * COARSE + cols : 2 * COARSE + cols + QUAD],
            None,
        )
        a_out[g] = a
        mixed[:, cols : cols + QUAD] = o
        stores.start(a_out, a_hbm, pl.ds(g, 1))
    stores.start(mixed, o_hbm)
    first = lax.axis_index("lat") % 2 == 0
    low = mm_tn(mixed[:, : COARSE // 2], cot) * 18432.0 ** (-0.5)
    high = mm_tn(mixed[:, COARSE // 2 :], cot) * 18432.0 ** (-0.5)
    own_half[...] = jnp.where(first, low, high).astype(BF)
    sent_half[...] = jnp.where(first, high, low).astype(BF)
    stores.finish()


def coarse_backward(
    place_of_parity, cot_hbm, proj_hbm, qkv_res, a_hbm, qkv_hbm, merged_hbm, fine_hbm, merge_hbm, o_hbm,
    out0, out1, out2, out3, out_hbm,
    cot_in, proj_w, qkv, a, qkv_w, merged, fine, merge_w, o, coarse_out, dqkv, in_sems, out_sems
):
    loads, stores = Loads(in_sems), Stores(out_sems)
    loads.add("cot", cot_hbm, cot_in)
    for i in range(2):
        loads.add("proj", proj_hbm, proj_w, chunk(i))
    loads.add("qkv", qkv_res, qkv)
    for g in range(4):
        loads.add("a", a_hbm, a, pl.ds(g, 1))
    loads.add("merged", merged_hbm, merged)
    loads.add("o", o_hbm, o)
    for i in range(3):
        loads.add("qkv_w", qkv_hbm, qkv_w, FULL, chunk(i, COARSE))
    loads.add("fine", fine_hbm, fine)
    for p in range(4):
        loads.add("merge", merge_hbm, merge_w, chunk(p))
    loads.start(0)
    loads.wait("cot")
    cot = cot_in[...].reshape(WIN, COARSE)
    cot_b = cot.astype(BF)
    grads = []
    for i in range(2):
        loads.wait("proj", i)
        grads.append(mm_nt(cot_b, proj_w[chunk(i)]).astype(BF))
    grad = jnp.concatenate(grads, axis=1)
    loads.wait("qkv")
    for g in range(4):
        loads.wait("a", g)
        cols = g * QUAD
        pulled = attend_pull(
            qkv[:, cols : cols + QUAD],
            qkv[:, COARSE + cols : COARSE + cols + QUAD],
            qkv[:, 2 * COARSE + cols : 2 * COARSE + cols + QUAD],
            a[g],
            grad[:, cols : cols + QUAD],
        )
        for i in range(3):
            dqkv[:, i * COARSE + cols : i * COARSE + cols + QUAD] = pulled[i]
    loads.wait("merged")
    loads.wait("o")
    merged_f = merged[...].astype(F32)
    full = (merged_f + mm(o[...], proj_w[...])).astype(BF)
    coarse_out[...] = full.astype(F32).reshape(coarse_out.shape).astype(BF)
    stores.start(coarse_out, out_hbm)
    dn = jnp.zeros((WIN, COARSE), F32)
    for i in range(3):
        loads.wait("qkv_w", i)
        dn = dn + mm_nt(dqkv[:, chunk(i, COARSE)], qkv_w[:, chunk(i, COARSE)])
    dn = dn.astype(BF).astype(F32)
    unit, scale = normed(merged_f)
    merged_grad = (cot + normed_pull(unit, scale, dn)).astype(BF)
    loads.wait("fine")
    units, scale = merge_unit([fine[p * WIN : (p + 1) * WIN].astype(F32) for p in range(4)])
    grads = []
    for p in range(4):
        loads.wait("merge", p)
        grads.append(mm_nt(merged_grad, merge_w[chunk(p)]).astype(BF).astype(F32))
    low = sum(jnp.sum(g, axis=-1, keepdims=True) for g in grads) / (4 * FINE)
    along = sum(jnp.sum(g * u, axis=-1, keepdims=True) for g, u in zip(grads, units)) / (4 * FINE)
    fine_grad = jnp.concatenate(
        [(scale * (g - low - u * along)).astype(BF) for g, u in zip(grads, units)], axis=0
    )
    split_pieces(moved_rows(place_of_parity, fine_grad, PACKED), (out0, out1, out2, out3))
    stores.finish()


def fine_backward(
    keep, beside, above, corner, window_at, place_of_window,
    x_hbm, qkv_res, a_hbm, att_hbm, slope_hbm, qkv_hbm, proj_hbm, up_hbm, down_hbm,
    out0, out1, out2, out3,
    x, qkv, a, att, slope, qkv_w, proj_w, up_w, down_w, dqkv, incoming, rounded, dn, grad,
    hidden_sems, window_sems, sems
):
    hidden_steps = HIDDEN // CHUNK

    def hidden_copies(c):
        cols = pl.ds(pl.multiple_of(c * CHUNK, CHUNK), CHUNK)
        return (
            pltpu.make_async_copy(down_hbm.at[cols], down_w.at[cols], hidden_sems.at[c, 0]),
            pltpu.make_async_copy(slope_hbm.at[:, cols], slope.at[:, cols], hidden_sems.at[c, 1]),
            pltpu.make_async_copy(up_hbm.at[:, cols], up_w.at[:, cols], hidden_sems.at[c, 2]),
        )

    def window_copies(w):
        pair = pl.ds(2 * w, 2)
        rows = pl.ds(pl.multiple_of(w * WIN, WIN), WIN)
        return (
            pltpu.make_async_copy(a_hbm.at[pair], a.at[pair], window_sems.at[w, 0]),
            pltpu.make_async_copy(qkv_res.at[rows], qkv.at[rows], window_sems.at[w, 1]),
        )

    att_copy = pltpu.make_async_copy(att_hbm, att, sems.at[0])
    proj_copy = pltpu.make_async_copy(proj_hbm, proj_w, sems.at[1])
    qkv_copy = pltpu.make_async_copy(qkv_hbm, qkv_w, sems.at[2])
    x_copy = pltpu.make_async_copy(x_hbm, x, sems.at[3])
    for c in range(2):
        for copy in hidden_copies(c):
            copy.start()
    arrived = moved_rows(window_at, joined_pieces((keep, beside, above, corner)), CELLS)
    incoming[...] = arrived
    rounded[...] = arrived.astype(BF)
    dn[...] = jnp.zeros_like(dn)

    @pl.loop(0, hidden_steps)
    def _(c):
        for copy in hidden_copies(c):
            copy.wait()

        @pl.when(c + 2 < hidden_steps)
        def _():
            for copy in hidden_copies(c + 2):
                copy.start()

        @pl.when(c + 2 == hidden_steps)
        def _():
            att_copy.start()
            proj_copy.start()

        @pl.when(c + 1 == hidden_steps)
        def _():
            for copy in (*window_copies(0), *window_copies(1)):
                copy.start()

        cols = pl.ds(pl.multiple_of(c * CHUNK, CHUNK), CHUNK)
        dh = mm_nt(rounded[...], down_w[cols]) * slope[:, cols].astype(F32)
        dn[...] += mm_nt(dh.astype(BF), up_w[:, cols])

    att_copy.wait()
    proj_copy.wait()
    unit, scale = normed(att[...])
    att_grad = incoming[...] + normed_pull(unit, scale, dn[...])
    incoming[...] = att_grad
    grad[...] = mm_nt(att_grad.astype(BF), proj_w[...]).astype(BF)

    @pl.loop(0, 4)
    def _(w):
        for copy in window_copies(w):
            copy.wait()

        @pl.when(w < 2)
        def _():
            for copy in window_copies(w + 2):
                copy.start()

        @pl.when(w == 2)
        def _():
            qkv_copy.start()
            x_copy.start()

        rows = pl.ds(pl.multiple_of(w * WIN, WIN), WIN)
        for g in range(2):
            cols = g * QUAD
            pulled = attend_pull(
                qkv[rows, cols : cols + QUAD],
                qkv[rows, FINE + cols : FINE + cols + QUAD],
                qkv[rows, 2 * FINE + cols : 2 * FINE + cols + QUAD],
                a[2 * w + g],
                grad[rows, cols : cols + QUAD],
            )
            for i in range(3):
                dqkv[rows, i * FINE + cols : i * FINE + cols + QUAD] = pulled[i]

    qkv_copy.wait()
    x_copy.wait()
    back = mm_nt(dqkv[...], qkv_w[...])
    unit, scale = normed(x[...].astype(F32))
    total = incoming[...] + normed_pull(unit, scale, back)
    split_pieces(
        moved_rows(place_of_window, total.astype(BF), PACKED), (out0, out1, out2, out3)
    )


def pack(cells, out0, out1, out2, out3):
    cell = lax.broadcasted_iota(jnp.int32, (1, CELLS), 1)
    line, kept = 2 * COLS, 2 * (COLS - HALF_LON)
    row = sum((cell >= line * r).astype(jnp.int32) for r in range(1, ROWS))
    across = cell - line * row
    rest, side = row - (ROWS - HALF_LAT), across - kept
    starts = [sum(PIECES[:i]) for i in range(4)]
    inner = jnp.where(side < 0, row * kept + across, starts[1] + row * (line - kept) + side)
    outer = jnp.where(
        side < 0, starts[2] + rest * kept + across, starts[3] + rest * (line - kept) + side
    )
    place = jnp.where(rest < 0, inner, outer)
    flat = cells[...].reshape(CELLS, FINE)
    split_pieces(moved_rows(place, flat, PACKED), (out0, out1, out2, out3))


def fetch(*refs):
    count = (len(refs) - 1) // 2
    copies = [
        pltpu.make_async_copy(refs[i], refs[count + i], refs[-1].at[i]) for i in range(count)
    ]
    for copy in copies:
        copy.start()
    for copy in copies:
        copy.wait()


def unpack(keep, beside, above, corner, cell_at, out_hbm, out, sems):
    stores = Stores(sems)
    pieces = joined_pieces((keep, beside, above, corner))
    cells = moved_rows(cell_at, pieces, CELLS)
    part = ROWS // 3
    for i in range(3):
        rows = cells[i * CELLS // 3 : (i + 1) * CELLS // 3]
        out[pl.ds(i * part, part)] = rows.reshape(part, COLS, 2, FINE)
        stores.start(out, out_hbm, pl.ds(i * part, part))
    stores.finish()


def pair_sum(own, other, out):
    out[...] = (own[...].astype(F32) + other[...].astype(F32)).astype(BF)


def share_sum(parts, after, out):
    total = parts[0].astype(F32)
    for i in range(1, parts.shape[0]):
        total = total + parts[i].astype(F32)
    total = total.astype(BF)
    for i in range(parts.shape[0]):
        out[i] = total


def write_half(half, rows, out_hbm, wide, sems):
    stores = Stores(sems)
    part = COARSE // 8
    for i in range(4):
        wide[pl.ds(i * part, part)] = half[pl.ds(i * part, part)].astype(F32)
        copy = pltpu.make_async_copy(
            wide.at[pl.ds(i * part, part)],
            out_hbm.at[pl.ds(pl.multiple_of(rows + i * part, part), part)],
            sems.at[i],
        )
        copy.start()
        stores.copies.append(copy)
    stores.finish()


def first_half(half, out_hbm, wide, sems):
    write_half(half, (lax.axis_index("lat") % 2) * (COARSE // 2), out_hbm, wide, sems)


def second_half(half, begun, out_hbm, wide, sems):
    write_half(half, (1 - lax.axis_index("lat") % 2) * (COARSE // 2), out_hbm, wide, sems)


def compiler_params():
    return pltpu.CompilerParams(vmem_limit_bytes=LIMIT)


def cost(micros, operands, outs):
    moved = sum(int(np.prod(o.shape)) * o.dtype.itemsize for o in jax.tree.leaves((operands, outs)))
    return pl.CostEstimate(
        flops=micros * 1153 * 10**6, bytes_accessed=moved, transcendentals=0
    )


def call(body, name, smem=(), vmem=(), hbm=(), outs=(), hbm_outs=(), scratch=(), sems=(), micros=1, after=()):
    hbm = [pltpu.with_memory_space_constraint(o, pltpu.HBM) for o in hbm]
    operands = [*smem, *vmem, *hbm]
    staged = [pltpu.VMEM(o.shape, o.dtype) for o in [*hbm, *hbm_outs]]
    waits = list(after)
    spaces = [pltpu.SMEM] * len(smem) + [pltpu.VMEM] * len(vmem) + [pltpu.HBM] * len(hbm)
    spaces += [pltpu.VMEM] * len(waits)
    results = [pltpu.VMEM] * len(outs) + [pltpu.HBM] * len(hbm_outs)
    return pl.pallas_call(
        body,
        name=name,
        out_shape=[
            *[pltpu.VMEM(o.shape, o.dtype) for o in outs], *[pltpu.HBM(o.shape, o.dtype) for o in hbm_outs]
        ],
        in_specs=[pl.BlockSpec(memory_space=space) for space in spaces],
        out_specs=[pl.BlockSpec(memory_space=space) for space in results],
        scratch_shapes=[*staged, *scratch] + ([pltpu.SemaphoreType.DMA(n if isinstance(n, tuple) else (n,)) for n in sems]),
        compiler_params=compiler_params(),
        cost_estimate=cost(micros, operands, [*outs, *hbm_outs]),
    )(*operands, *waits)


def fetched(name, arrays, after=None, micros=2):
    hbm = [pltpu.with_memory_space_constraint(array, pltpu.HBM) for array in arrays]
    spec = [pl.BlockSpec(memory_space=pltpu.HBM)] * len(hbm)
    waits = [] if after is None else [after]

    def body(*refs):
        fetch(*refs[: len(hbm)], *refs[len(hbm) + len(waits) :])

    return pl.pallas_call(
        body,
        name=name,
        out_shape=[pltpu.VMEM(array.shape, array.dtype) for array in arrays],
        in_specs=spec + [pl.BlockSpec(memory_space=pltpu.VMEM)] * len(waits),
        out_specs=[pl.BlockSpec(memory_space=pltpu.VMEM)] * len(hbm),
        scratch_shapes=[pltpu.SemaphoreType.DMA((len(hbm),))],
        compiler_params=compiler_params(),
        cost_estimate=cost(micros, arrays, arrays),
    )(*hbm, *waits)


def half_written(half, begun=None):
    half = half.reshape(COARSE // 2, COARSE)
    hbm = pl.BlockSpec(memory_space=pltpu.HBM)
    last = begun is not None
    return pl.pallas_call(
        second_half if last else first_half,
        name="second_half" if last else "first_half",
        out_shape=pltpu.HBM((COARSE, COARSE), F32),
        in_specs=[pl.BlockSpec(memory_space=pltpu.VMEM)] + [hbm] * last,
        out_specs=hbm,
        input_output_aliases={1: 0} if last else {},
        scratch_shapes=[pltpu.VMEM((COARSE // 2, COARSE), F32), pltpu.SemaphoreType.DMA((4,))],
        compiler_params=compiler_params(),
        cost_estimate=cost(2, half, half),
    )(half, *([begun] if last else []))


def piece_shapes():
    return [jax.ShapeDtypeStruct((room, FINE), BF) for room in PIECES]


def shifted(pieces, sign):
    lat_count, lon_count = lax.axis_size("lat"), lax.axis_size("lon")
    moved = [pieces[0]]
    for piece, (up, side) in zip(pieces[1:], ((0, 1), (1, 0), (1, 1))):
        pairs = []
        for i in range(lat_count):
            for j in range(lon_count):
                to = (i + sign * up) % lat_count, (j + sign * side) % lon_count
                pairs.append((i * lon_count + j, to[0] * lon_count + to[1]))
        moved.append(lax.ppermute(piece, BOTH, pairs))
    return moved


def swapped(values):
    return lax.ppermute(values, "lat", [(i, i ^ 1) for i in range(lax.axis_size("lat"))])


def same_core(values):
    lat_count, lon_count = lax.axis_size("lat"), lax.axis_size("lon")
    groups = [
        [i * lon_count + j for i in range(c, lat_count, 2) for j in range(lon_count)]
        for c in range(2)
    ]
    return lax.all_to_all(values, BOTH, 0, 0, tiled=True, axis_index_groups=groups)


def per_device(
    tokens, fine_qkv, fine_proj, fine_up, fine_down, merge_weight, coarse_qkv, coarse_proj, cotangent
):
    shape = jax.ShapeDtypeStruct
    pieces = call(
        pack, "pack_tokens", vmem=(tokens,),
        outs=piece_shapes(), micros=2,
    )
    *fine_weights, merge_w = fetched(
        "fetch_fine", (fine_qkv, fine_proj, fine_up, fine_down, merge_weight), after=pieces[3], micros=4
    )
    moved = shifted(pieces, 1)
    results = call(
        fine_forward,
        "fine_forward",
        vmem=(*moved, jnp.asarray(WINDOW_AT), jnp.asarray(PLACE_OF_WINDOW), *fine_weights),
        outs=piece_shapes(),
        hbm_outs=[
            shape((CELLS, FINE), BF), shape((CELLS, 3 * FINE), BF), shape((8, 4 * WIN, WIN), BF),
            shape((CELLS, FINE), F32), shape((CELLS, HIDDEN), BF),
        ],
        scratch=[pltpu.VMEM((CELLS, FINE), BF)],
        sems=(11,),
        micros=9,
    )
    pieces, saved = results[:4], results[4:]
    coarse_weights = fetched(
        "fetch_coarse", (coarse_qkv, cotangent), after=pieces[3], micros=3
    )
    moved = shifted(pieces, -1)
    own_half, sent_half, fine, merged, c_qkv, c_a, c_o = call(
        coarse_forward,
        "coarse_forward",
        vmem=(*moved, jnp.asarray(PARITY_AT), merge_w, *coarse_weights),
        outs=[shape((COARSE // 2, COARSE), BF)] * 2,
        hbm_outs=[
            shape((CELLS, FINE), BF), shape((WIN, COARSE), BF), shape((WIN, 3 * COARSE), BF),
            shape((4, 4 * WIN, WIN), BF), shape((WIN, COARSE), BF),
        ],
        sems=(8,),
        micros=7,
    )
    other_half = swapped(sent_half)
    (partial,) = call(
        pair_sum, "pair_sum", vmem=(own_half, other_half),
        outs=(shape((COARSE // 2, COARSE), BF),), micros=1,
    )
    sharers = lax.axis_size("lat") * lax.axis_size("lon") // 2
    shares = same_core(partial.reshape(sharers, COARSE // 2 // sharers, COARSE))
    *pieces, coarse_out = call(
        coarse_backward,
        "coarse_backward",
        vmem=(jnp.asarray(PLACE_OF_PARITY),),
        hbm=(cotangent, coarse_proj, c_qkv, c_a, coarse_qkv, merged, fine, merge_weight, c_o),
        outs=piece_shapes(),
        hbm_outs=(shape((6, 12, 2, COARSE), BF),),
        scratch=[pltpu.VMEM((WIN, 3 * COARSE), BF)],
        sems=(18, 1),
        micros=14,
    )
    moved = shifted(pieces, 1)
    (summed,) = call(
        share_sum, "share_sum", vmem=(shares,), outs=(shape(shares.shape, BF),), micros=1,
        after=pieces[3:],
    )
    half = same_core(summed)
    pieces = call(
        fine_backward,
        "fine_backward",
        vmem=(*moved, jnp.asarray(WINDOW_AT), jnp.asarray(PLACE_OF_WINDOW)),
        hbm=(*saved, fine_qkv, fine_proj, fine_up, fine_down),
        outs=piece_shapes(),
        scratch=[
            pltpu.VMEM((CELLS, 3 * FINE), BF), pltpu.VMEM((CELLS, FINE), F32), pltpu.VMEM((CELLS, FINE), BF),
            pltpu.VMEM((CELLS, FINE), F32), pltpu.VMEM((CELLS, FINE), BF),
        ],
        sems=((HIDDEN // CHUNK, 3), (4, 2), (4,)),
        micros=14,
    )
    begun = half_written(half)
    kept, *arrived = shifted(pieces, -1)
    half, begun, *arrived = lax.optimization_barrier((half, begun, *arrived))
    moved = [kept, *arrived]
    other = swapped(half)
    (input_grad,) = call(
        unpack, "unpack_grad", vmem=(*moved, jnp.asarray(CELL_AT)),
        hbm_outs=(shape((ROWS, COLS, 2, FINE), F32),), sems=(3,), micros=3,
    )
    proj_grad = half_written(other, begun)
    return coarse_out, input_grad, proj_grad


def solution(mesh):
    field = P("lat", "lon", None, None)
    return jax.shard_map(
        per_device,
        mesh=mesh,
        in_specs=(field, P(), P(), P(), P(), P(), P(), P(), field),
        out_specs=(field, field, P()),
        check_vma=False,
    )
```
